32 devices in a mesh: gx: 8 (over y, x, core), gy: 4 (over z).
Axes of the slice: x: 2, y: 2, z: 4, core: 2. Of those that a mesh axis runs over, the one named last changes fastest.
Arguments:
- right_side: float32 [3, 128, 64, 512], P(None, 'gx', 'gy'), may hold values from -8 to 8
- viscosity: float32 [128, 64, 512], P('gx', 'gy'), may hold values from 0.05 to 20
- reaction: float32 [128, 64, 512], P('gx', 'gy'), may hold values from 0.5 to 4
- agg_ids: int32 [128, 64, 512], P('gx', 'gy'), may hold values from 0 to 511
- owner_map: int32 [8, 4], P('gx', 'gy'), may hold values from 0 to 7, as said below
Outputs:
- velocity: float32 [3, 128, 64, 512], P(None, 'gx', 'gy')
- corrections: float32 [8, 4, 4, 3, 512], P('gx', 'gy')
The draws below stay inside these ranges and needn't reach their ends.
Inputs may be any that keep to these rules, and one draw needn't show every extreme that they name: `owner_map`: in every column along gy exactly one owner takes the blocks of 4 devices, its own among them; 3 devices own no block; every other device owns its own block.
All inputs are finite; a program needn't handle non-finite values.
Results may differ from the reference program's by a relative error of at most 0.0003.
Values sent between devices are 32-bit elements; how exact they have to be, the bound alone decides.
A program may use at most 64 MiB of HBM per device.

```python
import math
import jax
import jax.numpy as jnp
from jax import lax

CX = 16
CY = 16
CZ = 512
COMP = 3
NAGG = 512
NU = 3
MERGES = 3
MAXB = 4
NX = 128
NY = 64
NZ = 512
N_GX = 8
N_GY = 4


def draw_owner_map(key, part):
    key = jax.random.fold_in(key, 11)
    column_keys = jax.random.split(key, N_GY)
    ranks = jnp.arange(N_GX, dtype=jnp.int32)

    def one_column(column_key):
        order = jax.random.permutation(column_key, N_GX).astype(jnp.int32)
        target = jnp.where(ranks < MAXB, order[0], order)
        return jnp.zeros((N_GX,), jnp.int32).at[order].set(target)
    return jax.vmap(one_column)(column_keys).T


def place_ends(result, rng, low, largest):
    extent = result.shape
    index_at = [jax.random.randint(jax.random.fold_in(rng, axis), (), 0, extent[axis]) for axis in range(len(extent))]
    result = result.at[tuple(index_at)].set(low)
    longest = extent.index(max(extent))
    index_at[longest] = (index_at[longest] + 1) % extent[longest]
    return result.at[tuple(index_at)].set(largest)


def block_scale(stream_key, shape, pieces, smallest, top_value):
    factor_of, own = 1.0, jax.random.fold_in(stream_key, 6)
    for axis_at, parts in pieces:
        draws = jnp.exp(jax.random.uniform(jax.random.fold_in(own, axis_at), (parts,), jnp.float32, smallest / len(pieces), top_value / len(pieces)))
        factor_of = factor_of * jnp.repeat(draws, shape[axis_at] // parts).reshape([-1 if axis == axis_at else 1 for axis in range(len(shape))])
    return factor_of


def bell_draw(rng, dims, deviation, reach, pieces=(), kind=jnp.bfloat16):
    loudness = block_scale(rng, dims, pieces, -0.22, 0.18) if pieces else 1.0
    values = jax.random.normal(rng, dims, jnp.float32) * deviation * loudness
    return jnp.minimum(jnp.maximum(values, -reach), reach).astype(kind)


def setup_inputs(seed: int = 0) -> dict:
    seeds = jax.random.split(jax.random.key(seed), 6)
    return {
        "right_side": bell_draw(seeds[0], (COMP, NX, NY, NZ), 1.0, 8.0, ((1, 8), (2, 4)), jnp.float32),
        "viscosity": jnp.clip(jnp.exp(math.log(20.0) - 5.9914645 * jax.random.uniform(seeds[1], (NX, NY, NZ), jnp.float32) ** block_scale(seeds[1], (NX, NY, NZ), ((0, 8), (1, 4)), -0.2, 0.2)), 0.05, 20.0),
        "reaction": jnp.clip(jnp.exp(math.log(4.0) - 2.0794415 * jax.random.uniform(seeds[2], (NX, NY, NZ), jnp.float32) ** block_scale(seeds[2], (NX, NY, NZ), ((0, 8), (1, 4)), -0.2, 0.2)), 0.5, 4.0),
        "agg_ids": place_ends(jax.random.randint(seeds[3], (NX, NY, NZ), 0, NAGG), jax.random.fold_in(seeds[3], 1), 0, NAGG - 1).astype(jnp.int32),
        "owner_map": draw_owner_map(jax.random.fold_in(seeds[5], 71), 0),
    }


def face_weights(viscosity, reaction):
    padded_visc = jnp.pad(viscosity, 1)
    shifted = [padded_visc[2:, 1:-1, 1:-1], padded_visc[:-2, 1:-1, 1:-1], padded_visc[1:-1, 2:, 1:-1],
               padded_visc[1:-1, :-2, 1:-1], padded_visc[1:-1, 1:-1, 2:], padded_visc[1:-1, 1:-1, :-2]]
    weights = [0.5 * (viscosity + other) for other in shifted]
    diagonal = reaction + weights[0] + weights[1] + weights[2] + weights[3] + weights[4] + weights[5]
    return weights, diagonal


def apply_fine(padded_vel, field, weights, diagonal):
    beside = weights[0] * padded_vel[:, 2:, 1:-1, 1:-1] + weights[1] * padded_vel[:, :-2, 1:-1, 1:-1]
    beside = beside + weights[2] * padded_vel[:, 1:-1, 2:, 1:-1] + weights[3] * padded_vel[:, 1:-1, :-2, 1:-1]
    beside = beside + weights[4] * padded_vel[:, 1:-1, 1:-1, 2:] + weights[5] * padded_vel[:, 1:-1, 1:-1, :-2]
    return diagonal * field - beside


def coarse_apply(vector, coarse_diag):
    coupling = 0.2 * jnp.minimum(coarse_diag[..., :-1], coarse_diag[..., 1:])
    coupling = jnp.expand_dims(coupling, -2)
    zeros_end = jnp.zeros_like(vector[..., :1])
    upper = jnp.concatenate([coupling * vector[..., 1:], zeros_end], axis=-1)
    lower = jnp.concatenate([zeros_end, coupling * vector[..., :-1]], axis=-1)
    return jnp.expand_dims(coarse_diag, -2) * vector - (upper + lower)


def partner_rows(array, stride):
    count = array.shape[0]
    grouped = array.reshape((count // (2 * stride), 2, stride) + array.shape[1:])
    return grouped[:, ::-1].reshape(array.shape)


def all_levels(resid, coarse_diag):
    outputs = []
    for level in range(MERGES + 1):
        scaled = jnp.expand_dims(coarse_diag, -2)
        correction = 0.8 * resid / scaled
        correction = correction + 0.8 * (resid - coarse_apply(correction, coarse_diag)) / scaled
        outputs.append(correction)
        if level < MERGES:
            left_over = resid - coarse_apply(correction, coarse_diag)
            resid = left_over + partner_rows(left_over, 2 ** level)
            coarse_diag = coarse_diag + partner_rows(coarse_diag, 2 ** level)
    return outputs


def reference(right_side, viscosity, reaction, agg_ids, owner_map):
    weights, diagonal = face_weights(viscosity, reaction)
    widths = ((0, 0), (1, 1), (1, 1), (1, 1))
    velocity = jnp.zeros_like(right_side)
    for sweep in range(NU):
        image = apply_fine(jnp.pad(velocity, widths), velocity, weights, diagonal)
        velocity = velocity + 0.8 * (right_side - image) / diagonal
    resid = right_side - apply_fine(jnp.pad(velocity, widths), velocity, weights, diagonal)
    cells = CX * CY * CZ
    stacked = jnp.concatenate([resid, diagonal[None]], axis=0)
    stacked = stacked.reshape(COMP + 1, N_GX, CX, N_GY, CY, CZ).transpose(1, 3, 2, 4, 5, 0)
    stacked = stacked.reshape(N_GX * N_GY * cells, COMP + 1)
    local_ids = agg_ids.reshape(N_GX, CX, N_GY, CY, CZ).transpose(0, 2, 1, 3, 4).reshape(N_GX * N_GY, cells)
    block_base = (jnp.arange(N_GX * N_GY, dtype=jnp.int32) * NAGG)[:, None]
    global_ids = (local_ids + block_base).reshape(-1)
    block_sums = jax.ops.segment_sum(stacked, global_ids, num_segments=N_GX * N_GY * NAGG)
    block_sums = block_sums.reshape(N_GX, N_GY, NAGG, COMP + 1).transpose(0, 1, 3, 2)
    one_hot = (owner_map[:, :, None] == jnp.arange(N_GX, dtype=jnp.int32)[None, None, :]).astype(jnp.float32)
    owned = jnp.einsum('ijo,ijcn->ojcn', one_hot, block_sums, precision=lax.Precision.HIGHEST)
    outputs = all_levels(owned[:, :, :COMP], 1.0 + owned[:, :, COMP])
    return velocity, jnp.stack(outputs, axis=2)
```

```python
import functools

import jax
import jax.numpy as jnp
from jax import lax
from jax.experimental import pallas as pl
from jax.experimental.pallas import tpu as pltpu
from jax.sharding import PartitionSpec as P

COMP = 3
NAGG = 512
NU = 3
MERGES = 3
GROUP = 2**MERGES
LOW = 128
HIGH = NAGG // LOW
PACKED = 2 * (COMP + 1) * HIGH
SUMS = (COMP + 1) * HIGH
MESH = pl.DeviceIdType.MESH


def kernel(
    dims,
    rs_hbm,
    visc_hbm,
    reac_hbm,
    ids_hbm,
    own_ref,
    vel_hbm,
    cor_ref,
    rs,
    visc,
    diag,
    ids,
    weight,
    vel,
    res,
    halo_visc,
    pack_visc,
    halo_vel,
    pack_vel,
    face_w,
    part,
    gathered,
    local_sem,
    send_sem,
    recv_sem,
    all_send,
    all_recv,
):
    n_gx, n_gy, cx, cy, cz = dims
    rows = cx * cy
    gx, gy = lax.axis_index("gx"), lax.axis_index("gy")
    x_faces = (pl.ds(0, cy), pl.ds(rows - cy, cy))

    def face_rows(side):
        if side < 2:
            return [(x_faces[side], pl.ds(0, cy))]
        return [
            (pl.ds(at * cy + (cy - 1 if side == 3 else 0), 1), pl.ds(at, 1)) for at in range(cx)
        ]

    has = (gx > 0, gx < n_gx - 1, gy > 0, gy < n_gy - 1)
    targets = ((gx - 1, gy), (gx + 1, gy), (gx, gy - 1), (gx, gy + 1))

    loads = [
        pltpu.make_async_copy(src, dst, local_sem.at[at])
        for at, (src, dst) in enumerate(
            ((visc_hbm, visc), (reac_hbm, diag), (rs_hbm, rs), (ids_hbm, ids))
        )
    ]
    for load in loads:
        load.start()

    barrier = pltpu.get_barrier_semaphore()
    for step in range(1, n_gx):
        pl.semaphore_signal(
            barrier, inc=1, device_id=(lax.rem(gx + step, n_gx), gy), device_id_type=MESH
        )
    for side in (2, 3):

        @pl.when(has[side])
        def _():
            pl.semaphore_signal(barrier, inc=1, device_id=targets[side], device_id_type=MESH)

    loads[0].wait()
    for side in (2, 3):
        for here, there in face_rows(side):
            pack_visc[side - 2, there, :] = visc[here, :]
    waits = (n_gx - 1) + has[2].astype(jnp.int32) + has[3].astype(jnp.int32)
    pl.semaphore_wait(barrier, waits)

    def face_copy(turn, side):
        other = side ^ 1
        if turn == 0:
            src = visc.at[x_faces[side], :] if side < 2 else pack_visc.at[side - 2]
            dst = halo_visc.at[other]
        else:
            src = vel.at[turn - 1, :, x_faces[side], :] if side < 2 else pack_vel.at[turn - 1, side - 2]
            dst = halo_vel.at[turn - 1, other]
        return pltpu.make_async_remote_copy(
            src_ref=src,
            dst_ref=dst,
            send_sem=send_sem.at[turn, side],
            recv_sem=recv_sem.at[turn, other],
            device_id=targets[side],
            device_id_type=MESH,
        )

    def send_faces(turn):
        for side in range(4):

            @pl.when(has[side])
            def _():
                face_copy(turn, side).start()

    def with_faces(turn, work):
        for side in range(4):

            @pl.when(has[side])
            def _():
                face_copy(turn, side ^ 1).wait_recv()
                work(side)

    def drain(turn):
        for side in range(4):

            @pl.when(has[side])
            def _():
                face_copy(turn, side).wait_send()

    send_faces(0)
    shape = (cy, cz)
    row_at = lax.broadcasted_iota(jnp.int32, shape, 0)
    lane_at = lax.broadcasted_iota(jnp.int32, shape, 1)
    no_high_y, no_low_y = row_at == cy - 1, row_at == 0
    no_high_z, no_low_z = lane_at == cz - 1, lane_at == 0

    def plane(at):
        return pl.ds(pl.multiple_of(at * cy, cy), cy)

    def beside_in(array):
        return (
            pltpu.roll(array, cy - 1, 0),
            pltpu.roll(array, 1, 0),
            pltpu.roll(array, cz - 1, 1),
            pltpu.roll(array, 1, 1),
        )

    drops = (no_high_y, no_low_y, no_high_z, no_low_z)

    def over_planes(work):
        work(0, False, True)

        @pl.loop(1, cx - 1)
        def _(at):
            work(at, True, True)

        work(cx - 1, True, False)

    loads[1].wait()

    def sum_weights(at, low, high):
        here = visc[plane(at), :]
        total = jnp.zeros(shape, jnp.float32)
        for other, drop in zip(beside_in(here), drops):
            total += jnp.where(drop, 0.0, other)
        if high:
            total += visc[plane(at + 1), :]
        if low:
            total += visc[plane(at - 1), :]
        diag[plane(at), :] = diag[plane(at), :] + 3.0 * here + 0.5 * total

    over_planes(sum_weights)

    def add_visc(side):
        for here, there in face_rows(side):
            diag[here, :] = diag[here, :] + 0.5 * halo_visc[side, there, :]

    with_faces(0, add_visc)
    loads[2].wait()

    def scale_weights(at, low, high):
        here = visc[plane(at), :]
        scale = 0.8 / diag[plane(at), :]
        for comp in range(COMP):
            vel[0, comp, plane(at), :] = scale * rs[comp, plane(at), :]
        half = 0.5 * scale
        if high:
            weight[0, plane(at), :] = half * (here + visc[plane(at + 1), :])
        if low:
            weight[1, plane(at), :] = half * (here + visc[plane(at - 1), :])
        for which, (other, drop) in enumerate(zip(beside_in(here), drops)):
            weight[2 + which, plane(at), :] = jnp.where(drop, 0.0, half * (here + other))

    over_planes(scale_weights)

    def pack(turn):
        for side in (2, 3):
            for here, there in face_rows(side):
                for comp in range(COMP):
                    pack_vel[turn - 1, side - 2, comp, there, :] = vel[turn - 1, comp, here, :]

    pack(1)
    send_faces(1)
    for side in range(4):

        @pl.when(has[side])
        def _():
            for here, there in face_rows(side):
                face_w[side, there, :] = (
                    0.4 / diag[here, :] * (visc[here, :] + halo_visc[side, there, :])
                )

    def from_beside(turn, comp, at, low, high):
        here = vel[turn, comp, plane(at), :]
        total = jnp.zeros(shape, jnp.float32)
        for which, other in enumerate(beside_in(here)):
            total += weight[2 + which, plane(at), :] * other
        if high:
            total += weight[0, plane(at), :] * vel[turn, comp, plane(at + 1), :]
        if low:
            total += weight[1, plane(at), :] * vel[turn, comp, plane(at - 1), :]
        return here, total

    for turn in range(1, NU):

        def sweep(at, low, high):
            for comp in range(COMP):
                here, total = from_beside(turn - 1, comp, at, low, high)
                vel[turn, comp, plane(at), :] = vel[0, comp, plane(at), :] + 0.2 * here + total

        over_planes(sweep)

        def add_vel(side):
            for here, there in face_rows(side):
                ratio = face_w[side, there, :]
                for comp in range(COMP):
                    vel[turn, comp, here, :] = (
                        vel[turn, comp, here, :] + ratio * halo_vel[turn - 1, side, comp, there, :]
                    )

        with_faces(turn, add_vel)
        pack(turn + 1)
        send_faces(turn + 1)

    store = pltpu.make_async_copy(vel.at[NU - 1], vel_hbm, local_sem.at[4])
    store.start()

    def residual(at, low, high):
        scale = 1.25 * diag[plane(at), :]
        for comp in range(COMP):
            here, total = from_beside(NU - 1, comp, at, low, high)
            res[comp, plane(at), :] = scale * (vel[0, comp, plane(at), :] - 0.8 * here + total)

    over_planes(residual)
    loads[3].wait()

    high_at = lax.broadcasted_iota(jnp.int32, (8, cz), 0)
    first_half = high_at < HIGH
    high_at = lax.rem(high_at, HIGH)
    low_at = lax.broadcasted_iota(jnp.int32, (LOW, cz), 0).astype(jnp.float32).astype(jnp.bfloat16)
    one, zero = jnp.ones((), jnp.bfloat16), jnp.zeros((), jnp.bfloat16)

    def add_row(total, row):
        def spread(ref_row):
            return jnp.broadcast_to(ref_row, (8, cz))

        labels = spread(ids[pl.ds(row, 1), :])
        is_high = lax.div(labels, LOW) == high_at
        low = lax.rem(labels, LOW).astype(jnp.float32)
        low = jnp.concatenate([low, low], axis=0).astype(jnp.bfloat16)
        low = jnp.concatenate([low] * (LOW // 16), axis=0)
        table = jnp.where(low == low_at, one, zero)
        values = [spread(res[comp, pl.ds(row, 1), :]) for comp in range(COMP)]
        values.append(spread(diag[pl.ds(row, 1), :]))
        pairs = [
            jnp.where(is_high, jnp.where(first_half, values[at], values[at + 1]), 0.0)
            for at in (0, 2)
        ]
        whole = jnp.concatenate(pairs, axis=0)
        coarse = whole.astype(jnp.bfloat16)
        fine = (whole - coarse.astype(jnp.float32)).astype(jnp.bfloat16)
        parts = jnp.concatenate([coarse, fine], axis=0)
        return total + lax.dot_general(
            parts, table, (((1,), (1,)), ((), ())), preferred_element_type=jnp.float32
        )

    def add_rows(total, start, within):
        def body(at, carried):
            for row in within:
                carried = add_row(carried, at * cy + row)
            return carried

        return lax.fori_loop(start[0], start[1], body, total)

    total = jnp.zeros((PACKED, LOW), jnp.float32)
    total = add_rows(total, (1, cx - 1), range(1, cy - 1))

    def add_res(side):
        for here, there in face_rows(side):
            scale = 1.25 * diag[here, :] * face_w[side, there, :]
            for comp in range(COMP):
                res[comp, here, :] = (
                    res[comp, here, :] + scale * halo_vel[NU - 1, side, comp, there, :]
                )

    with_faces(NU, add_res)
    total = add_rows(total, (1, cx - 1), (0, cy - 1))
    total = add_rows(total, (0, 1), range(cy))
    total = add_rows(total, (cx - 1, cx), range(cy))

    part[0:SUMS, :] = total[:SUMS] + total[SUMS:]
    part[SUMS : SUMS + 8, :] = jnp.full((8, LOW), own_ref[0, 0], jnp.int32).astype(jnp.float32)

    def share(step):
        return pltpu.make_async_remote_copy(
            src_ref=part,
            dst_ref=gathered.at[step],
            send_sem=all_send.at[step],
            recv_sem=all_recv.at[step],
            device_id=(lax.rem(gx + step, n_gx), gy),
            device_id_type=MESH,
        )

    for step in range(1, n_gx):
        share(step).start()

    base = lax.div(gx, GROUP) * GROUP
    member = lax.broadcasted_iota(jnp.int32, (GROUP, LOW), 0)
    owner_of = (base + member).astype(jnp.float32)
    tiles = [jnp.zeros((GROUP, LOW), jnp.float32) for _ in range(SUMS)]
    for step in range(n_gx):
        if step:
            share(step).wait_recv()
        source = gathered.at[step] if step else part
        mine = source[SUMS : SUMS + 8, :] == owner_of
        for at in range(SUMS):
            row = jnp.broadcast_to(source[at : at + 1, :], (GROUP, LOW))
            tiles[at] = tiles[at] + jnp.where(mine, row, 0.0)
    owned = [
        jnp.concatenate(tiles[comp * HIGH : (comp + 1) * HIGH], axis=1) for comp in range(COMP + 1)
    ]
    coarse_res, coarse_diag = owned[:COMP], 1.0 + owned[COMP]
    lane = lax.broadcasted_iota(jnp.int32, (GROUP, NAGG), 1)
    member = lax.broadcasted_iota(jnp.int32, (GROUP, NAGG), 0)
    own_row = member == gx - base

    def partner(value, level):
        apart = 2**level
        odd = lax.rem(lax.div(member, apart), 2) == 1
        return jnp.where(
            odd, pltpu.roll(value, apart, 0), pltpu.roll(value, GROUP - apart, 0)
        )

    for level in range(MERGES + 1):
        coupling = 0.2 * jnp.minimum(coarse_diag, pltpu.roll(coarse_diag, NAGG - 1, 1))
        coupling = jnp.where(lane == NAGG - 1, 0.0, coupling)
        below = pltpu.roll(coupling, 1, 1)
        scale = 0.8 / coarse_diag

        def left(resid, vector):
            image = (
                coarse_diag * vector
                - coupling * pltpu.roll(vector, NAGG - 1, 1)
                - below * pltpu.roll(vector, 1, 1)
            )
            return resid - image

        merged = []
        for comp in range(COMP):
            resid = coarse_res[comp]
            error = scale * resid
            error = error + scale * left(resid, error)
            cor_ref[0, 0, level, comp : comp + 1, :] = jnp.sum(
                jnp.where(own_row, error, 0.0), axis=0, keepdims=True
            )
            if level < MERGES:
                rest = left(resid, error)
                merged.append(rest + partner(rest, level))
        if level < MERGES:
            coarse_res = merged
            coarse_diag = coarse_diag + partner(coarse_diag, level)

    for turn in range(NU + 1):
        drain(turn)
    for step in range(1, n_gx):
        share(step).wait_send()
    store.wait()


def shards(n_gx, n_gy, right_side, viscosity, reaction, agg_ids, owner_map):
    comp, cx, cy, cz = right_side.shape
    rows = cx * cy
    whole = (rows, cz)
    face = (cx, cz)
    hbm = pl.BlockSpec(memory_space=pl.ANY)
    f32 = jnp.float32
    velocity, levels = pl.pallas_call(
        functools.partial(kernel, (n_gx, n_gy, cx, cy, cz)),
        out_shape=(
            jax.ShapeDtypeStruct((comp,) + whole, f32),
            jax.ShapeDtypeStruct((1, 1, MERGES + 1, comp, NAGG), f32),
        ),
        in_specs=[hbm] * 4 + [pl.BlockSpec(memory_space=pltpu.SMEM)],
        out_specs=(hbm, pl.BlockSpec(memory_space=pltpu.VMEM)),
        scratch_shapes=[
            pltpu.VMEM((comp,) + whole, f32),
            pltpu.VMEM(whole, f32),
            pltpu.VMEM(whole, f32),
            pltpu.VMEM(whole, jnp.int32),
            pltpu.VMEM((6,) + whole, f32),
            pltpu.VMEM((NU, comp) + whole, f32),
            pltpu.VMEM((comp,) + whole, f32),
            pltpu.VMEM((4,) + face, f32),
            pltpu.VMEM((2,) + face, f32),
            pltpu.VMEM((NU, 4, comp) + face, f32),
            pltpu.VMEM((NU, 2, comp) + face, f32),
            pltpu.VMEM((4,) + face, f32),
            pltpu.VMEM((SUMS + 8, LOW), f32),
            pltpu.VMEM((n_gx, SUMS + 8, LOW), f32),
            pltpu.SemaphoreType.DMA((5,)),
            pltpu.SemaphoreType.DMA((NU + 1, 4)),
            pltpu.SemaphoreType.DMA((NU + 1, 4)),
            pltpu.SemaphoreType.DMA((n_gx,)),
            pltpu.SemaphoreType.DMA((n_gx,)),
        ],
        compiler_params=pltpu.CompilerParams(
            collective_id=0, has_side_effects=True, vmem_limit_bytes=40 * 2**20
        ),
    )(
        right_side.reshape((comp,) + whole),
        viscosity.reshape(whole),
        reaction.reshape(whole),
        agg_ids.reshape(whole),
        owner_map,
    )
    return velocity.reshape(right_side.shape), levels


def solution(mesh):
    return jax.shard_map(
        functools.partial(shards, mesh.shape["gx"], mesh.shape["gy"]),
        mesh=mesh,
        in_specs=(
            P(None, "gx", "gy", None),
            P("gx", "gy", None),
            P("gx", "gy", None),
            P("gx", "gy", None),
            P("gx", "gy"),
        ),
        out_specs=(P(None, "gx", "gy", None), P("gx", "gy", None, None, None)),
        check_vma=False,
    )
```

```python
import functools

import jax
import jax.numpy as jnp
from jax import lax
from jax.experimental import pallas as pl
from jax.experimental.pallas import tpu as pltpu
from jax.sharding import PartitionSpec as P

COMP = 3
NAGG = 512
NU = 3
MERGES = 3
GROUP = 2**MERGES
LANES = 128
LOW = 128
HIGH = NAGG // LOW
PACKED = 2 * (COMP + 1) * HIGH
SUMS = (COMP + 1) * HIGH
MESH = pl.DeviceIdType.MESH


def kernel(
    dims,
    rs_hbm,
    visc_hbm,
    reac_hbm,
    ids_hbm,
    own_ref,
    vel_hbm,
    cor_ref,
    rs,
    visc,
    diag,
    ids,
    low_ids,
    weight,
    vel,
    res,
    halo_visc,
    pack_visc,
    halo_vel,
    pack_vel,
    face_w,
    part,
    gathered,
    load_sem,
    store_sem,
    send_sem,
    recv_sem,
    all_send,
    all_recv,
):
    n_gx, n_gy, cx, cy, cz = dims
    rows = cx * cy
    tiles_z = cz // LANES
    gx, gy = lax.axis_index("gx"), lax.axis_index("gy")
    has = (gx > 0, gx < n_gx - 1, gy > 0, gy < n_gy - 1)
    targets = ((gx - 1, gy), (gx + 1, gy), (gx, gy - 1), (gx, gy + 1))

    def face(side, before=0):
        if side < 2:
            return pl.ds(before + (rows - cy if side else 0), cy)
        return pl.ds(before + (cy - 1 if side == 3 else 0), cx, stride=cy)

    block = pl.ds(cy, rows)
    sources = (visc_hbm, reac_hbm, ids_hbm, rs_hbm)
    loads = []
    for which, src in enumerate(sources):
        pieces = []
        for tile in range(tiles_z):
            lanes = pl.ds(tile * LANES, LANES)
            if which == 0:
                ends = src.at[:, lanes], visc.at[tile, block, :]
            elif which == 3:
                ends = src.at[:, :, lanes], rs.at[:, tile]
            else:
                ends = src.at[:, lanes], (diag if which == 1 else ids).at[tile]
            pieces.append(pltpu.make_async_copy(*ends, load_sem.at[which, tile]))
        loads.append(pieces)
    for pieces in loads:
        for piece in pieces:
            piece.start()

    def arrived(which):
        for piece in loads[which]:
            piece.wait()

    barrier = pltpu.get_barrier_semaphore()
    for step in range(1, n_gx):
        pl.semaphore_signal(
            barrier, inc=1, device_id=(lax.rem(gx + step, n_gx), gy), device_id_type=MESH
        )
    for side in (2, 3):

        @pl.when(has[side])
        def _():
            pl.semaphore_signal(barrier, inc=1, device_id=targets[side], device_id_type=MESH)

    empty = jnp.zeros((cy, LANES), jnp.float32)
    for tile in range(tiles_z):
        for rim in (0, rows + cy):
            visc[tile, rim : rim + cy, :] = empty
            for turn in range(NU):
                for comp in range(COMP):
                    vel[turn, comp, tile, rim : rim + cy, :] = empty

    arrived(0)
    for side in (2, 3):
        for tile in range(tiles_z):
            pack_visc[side - 2, tile] = visc[tile, face(side, cy), :]
    waits = (n_gx - 1) + has[2].astype(jnp.int32) + has[3].astype(jnp.int32)
    pl.semaphore_wait(barrier, waits)

    def face_copy(turn, side):
        other = side ^ 1
        if turn == 0:
            src = visc.at[:, face(side, cy), :] if side < 2 else pack_visc.at[side - 2]
            dst = halo_visc.at[other]
        else:
            src = (
                vel.at[turn - 1, :, :, face(side, cy), :]
                if side < 2
                else pack_vel.at[turn - 1, side - 2]
            )
            dst = halo_vel.at[turn - 1, other]
        return pltpu.make_async_remote_copy(
            src_ref=src,
            dst_ref=dst,
            send_sem=send_sem.at[turn, side],
            recv_sem=recv_sem.at[turn, other],
            device_id=targets[side],
            device_id_type=MESH,
        )

    def send_faces(turn):
        for side in range(4):

            @pl.when(has[side])
            def _():
                if turn and side >= 2:
                    for comp in range(COMP):
                        for tile in range(tiles_z):
                            pack_vel[turn - 1, side - 2, comp, tile] = vel[
                                turn - 1, comp, tile, face(side, cy), :
                            ]
                face_copy(turn, side).start()

    def with_faces(turn, work):
        for side in range(4):

            @pl.when(has[side])
            def _():
                face_copy(turn, side ^ 1).wait_recv()
                for tile in range(tiles_z):
                    work(side, tile)

    def drain(turn):
        for side in range(4):

            @pl.when(has[side])
            def _():
                face_copy(turn, side).wait_send()

    send_faces(0)
    shape = (cy, LANES)
    row_at = lax.broadcasted_iota(jnp.int32, shape, 0)
    lane_at = lax.broadcasted_iota(jnp.int32, shape, 1)
    no_high_y, no_low_y = row_at == cy - 1, row_at == 0
    last_lane, first_lane = lane_at == LANES - 1, lane_at == 0

    def plane(at, before=0):
        return pl.ds(pl.multiple_of(at * cy, cy) + before, cy)

    def beside_z(pieces, tile):
        here = pieces[tile]
        above = jnp.where(first_lane, pieces[(tile + 1) % tiles_z], here)
        under = jnp.where(last_lane, pieces[tile - 1], here)
        return pltpu.roll(above, LANES - 1, 1), pltpu.roll(under, 1, 1)

    def visc_beside(at, tile, pieces):
        high_z, low_z = beside_z(pieces, tile)
        if tile == tiles_z - 1:
            high_z = jnp.where(last_lane, 0.0, high_z)
        if tile == 0:
            low_z = jnp.where(first_lane, 0.0, low_z)
        return (
            visc[tile, plane(at, 2 * cy), :],
            visc[tile, plane(at), :],
            jnp.where(no_high_y, 0.0, visc[tile, plane(at, cy + 1), :]),
            jnp.where(no_low_y, 0.0, visc[tile, plane(at, cy - 1), :]),
            high_z,
            low_z,
        )

    arrived(1)

    @pl.loop(0, cx)
    def _(at):
        pieces = [visc[tile, plane(at, cy), :] for tile in range(tiles_z)]
        for tile in range(tiles_z):
            total = functools.reduce(jnp.add, visc_beside(at, tile, pieces))
            diag[tile, plane(at), :] = (
                diag[tile, plane(at), :] + 3.0 * pieces[tile] + 0.5 * total
            )

    arrived(2)

    @pl.loop(0, cx)
    def _(at):
        for tile in range(tiles_z):
            label = ids[tile, plane(at), :]
            low_ids[tile, plane(at), :] = (label & (LOW - 1)).astype(jnp.float32)
            ids[tile, plane(at), :] = lax.shift_right_logical(label, LOW.bit_length() - 1)

    def add_visc(side, tile):
        diag[tile, face(side), :] = diag[tile, face(side), :] + 0.5 * halo_visc[side, tile]

    with_faces(0, add_visc)
    arrived(3)

    @pl.loop(0, cx)
    def _(at):
        pieces = [visc[tile, plane(at, cy), :] for tile in range(tiles_z)]
        for tile in range(tiles_z):
            here = pieces[tile]
            scale = 0.8 / diag[tile, plane(at), :]
            for comp in range(COMP):
                vel[0, comp, tile, plane(at, cy), :] = scale * rs[comp, tile, plane(at), :]
            half = 0.5 * scale
            found = visc_beside(at, tile, pieces)
            drops = [None, None, no_high_y, no_low_y, None, None]
            if tile == tiles_z - 1:
                drops[4] = last_lane
            if tile == 0:
                drops[5] = first_lane
            for which, (other, drop) in enumerate(zip(found, drops)):
                ratio = half * (here + other)
                if drop is not None:
                    ratio = jnp.where(drop, 0.0, ratio)
                weight[which, tile, plane(at), :] = ratio

    send_faces(1)
    for side in range(4):

        @pl.when(has[side])
        def _():
            for tile in range(tiles_z):
                face_w[side, tile] = (
                    0.4
                    / diag[tile, face(side), :]
                    * (visc[tile, face(side, cy), :] + halo_visc[side, tile])
                )

    def from_beside(turn, at, write):
        pieces = [
            [vel[turn, comp, tile, plane(at, cy), :] for tile in range(tiles_z)]
            for comp in range(COMP)
        ]
        for tile in range(tiles_z):
            ratios = [weight[which, tile, plane(at), :] for which in range(6)]
            for comp in range(COMP):
                high_z, low_z = beside_z(pieces[comp], tile)
                total = ratios[0] * vel[turn, comp, tile, plane(at, 2 * cy), :]
                total += ratios[1] * vel[turn, comp, tile, plane(at), :]
                total += ratios[2] * vel[turn, comp, tile, plane(at, cy + 1), :]
                total += ratios[3] * vel[turn, comp, tile, plane(at, cy - 1), :]
                total += ratios[4] * high_z + ratios[5] * low_z
                write(comp, tile, pieces[comp][tile], total)

    for turn in range(1, NU):

        @pl.loop(0, cx)
        def _(at):
            def write(comp, tile, here, total):
                first = vel[0, comp, tile, plane(at, cy), :]
                vel[turn, comp, tile, plane(at, cy), :] = first + 0.2 * here + total

            from_beside(turn - 1, at, write)

        def add_vel(side, tile):
            ratio = face_w[side, tile]
            for comp in range(COMP):
                vel[turn, comp, tile, face(side, cy), :] = (
                    vel[turn, comp, tile, face(side, cy), :]
                    + ratio * halo_vel[turn - 1, side, comp, tile]
                )

        with_faces(turn, add_vel)
        send_faces(turn + 1)

    stores = [
        pltpu.make_async_copy(
            vel.at[NU - 1, :, tile, block, :],
            vel_hbm.at[:, :, pl.ds(tile * LANES, LANES)],
            store_sem.at[tile],
        )
        for tile in range(tiles_z)
    ]
    for store in stores:
        store.start()

    @pl.loop(0, cx)
    def _(at):
        def write(comp, tile, here, total):
            scale = 1.25 * diag[tile, plane(at), :]
            first = vel[0, comp, tile, plane(at, cy), :]
            res[comp, tile, plane(at), :] = scale * (first - 0.8 * here + total)

        from_beside(NU - 1, at, write)

    high_at = lax.broadcasted_iota(jnp.int32, (8, cz), 0)
    first_half = high_at < HIGH
    high_at = high_at & (HIGH - 1)
    low_at = lax.broadcasted_iota(jnp.int32, (LOW, cz), 0).astype(jnp.float32).astype(jnp.bfloat16)
    one, zero = jnp.ones((), jnp.bfloat16), jnp.zeros((), jnp.bfloat16)

    def add_row(total, row):
        def spread(*where):
            return jnp.concatenate(
                [
                    jnp.broadcast_to(where[0][(*where[1:], tile, pl.ds(row, 1))], (8, LANES))
                    for tile in range(tiles_z)
                ],
                axis=1,
            )

        is_high = spread(ids) == high_at
        low = spread(low_ids)
        low = jnp.concatenate([low, low], axis=0).astype(jnp.bfloat16)
        low = jnp.concatenate([low] * (LOW // 16), axis=0)
        table = jnp.where(low == low_at, one, zero)
        values = [spread(res, comp) for comp in range(COMP)] + [spread(diag)]
        pairs = [
            jnp.where(is_high, jnp.where(first_half, values[at], values[at + 1]), 0.0)
            for at in (0, 2)
        ]
        whole = jnp.concatenate(pairs, axis=0)
        coarse = whole.astype(jnp.bfloat16)
        fine = (whole - coarse.astype(jnp.float32)).astype(jnp.bfloat16)
        parts = jnp.concatenate([coarse, fine], axis=0)
        return total + lax.dot_general(
            parts, table, (((1,), (1,)), ((), ())), preferred_element_type=jnp.float32
        )

    def add_rows(total, start, within):
        def body(at, carried):
            for row in within:
                carried = add_row(carried, at * cy + row)
            return carried

        return lax.fori_loop(start[0], start[1], body, total)

    total = jnp.zeros((PACKED, LOW), jnp.float32)
    total = add_rows(total, (1, cx - 1), range(1, cy - 1))

    def add_res(side, tile):
        scale = 1.25 * diag[tile, face(side), :] * face_w[side, tile]
        for comp in range(COMP):
            res[comp, tile, face(side), :] = (
                res[comp, tile, face(side), :] + scale * halo_vel[NU - 1, side, comp, tile]
            )

    with_faces(NU, add_res)
    total = add_rows(total, (1, cx - 1), (0, cy - 1))
    total = add_rows(total, (0, 1), range(cy))
    total = add_rows(total, (cx - 1, cx), range(cy))

    part[0:SUMS, :] = total[:SUMS] + total[SUMS:]
    part[SUMS : SUMS + 8, :] = jnp.full((8, LOW), own_ref[0, 0], jnp.int32).astype(jnp.float32)

    def share(step):
        return pltpu.make_async_remote_copy(
            src_ref=part,
            dst_ref=gathered.at[step],
            send_sem=all_send.at[step],
            recv_sem=all_recv.at[step],
            device_id=(lax.rem(gx + step, n_gx), gy),
            device_id_type=MESH,
        )

    for step in range(1, n_gx):
        share(step).start()

    base = lax.div(gx, GROUP) * GROUP
    member = lax.broadcasted_iota(jnp.int32, (GROUP, LOW), 0)
    owner_of = (base + member).astype(jnp.float32)
    tiles = [jnp.zeros((GROUP, LOW), jnp.float32) for _ in range(SUMS)]
    for step in range(n_gx):
        if step:
            share(step).wait_recv()
        source = gathered.at[step] if step else part
        mine = source[SUMS : SUMS + 8, :] == owner_of
        for at in range(SUMS):
            row = jnp.broadcast_to(source[at : at + 1, :], (GROUP, LOW))
            tiles[at] = tiles[at] + jnp.where(mine, row, 0.0)
    owned = [
        jnp.concatenate(tiles[comp * HIGH : (comp + 1) * HIGH], axis=1) for comp in range(COMP + 1)
    ]
    coarse_res, coarse_diag = owned[:COMP], 1.0 + owned[COMP]
    lane = lax.broadcasted_iota(jnp.int32, (GROUP, NAGG), 1)
    member = lax.broadcasted_iota(jnp.int32, (GROUP, NAGG), 0)
    own_row = member == gx - base

    def partner(value, level):
        apart = 2**level
        odd = lax.rem(lax.div(member, apart), 2) == 1
        return jnp.where(
            odd, pltpu.roll(value, apart, 0), pltpu.roll(value, GROUP - apart, 0)
        )

    for level in range(MERGES + 1):
        coupling = 0.2 * jnp.minimum(coarse_diag, pltpu.roll(coarse_diag, NAGG - 1, 1))
        coupling = jnp.where(lane == NAGG - 1, 0.0, coupling)
        below = pltpu.roll(coupling, 1, 1)
        scale = 0.8 / coarse_diag

        def left(resid, vector):
            image = (
                coarse_diag * vector
                - coupling * pltpu.roll(vector, NAGG - 1, 1)
                - below * pltpu.roll(vector, 1, 1)
            )
            return resid - image

        merged = []
        for comp in range(COMP):
            resid = coarse_res[comp]
            error = scale * resid
            error = error + scale * left(resid, error)
            cor_ref[0, 0, comp, level : level + 1, :] = jnp.sum(
                jnp.where(own_row, error, 0.0), axis=0, keepdims=True
            )
            if level < MERGES:
                rest = left(resid, error)
                merged.append(rest + partner(rest, level))
        if level < MERGES:
            coarse_res = merged
            coarse_diag = coarse_diag + partner(coarse_diag, level)

    for turn in range(NU + 1):
        drain(turn)
    for step in range(1, n_gx):
        share(step).wait_send()
    for store in stores:
        store.wait()


def shards(n_gx, n_gy, right_side, viscosity, reaction, agg_ids, owner_map):
    comp, cx, cy, cz = right_side.shape
    rows = cx * cy
    whole = (rows, cz)
    tiles_z = cz // LANES
    inside = (tiles_z, rows, LANES)
    rimmed = (tiles_z, rows + 2 * cy, LANES)
    face = (tiles_z, cx, LANES)
    hbm = pl.BlockSpec(memory_space=pltpu.HBM)
    f32 = jnp.float32
    velocity, levels = pl.pallas_call(
        functools.partial(kernel, (n_gx, n_gy, cx, cy, cz)),
        out_shape=(
            jax.ShapeDtypeStruct((comp,) + whole, f32),
            jax.ShapeDtypeStruct((1, 1, comp, MERGES + 1, NAGG), f32),
        ),
        in_specs=[hbm] * 4 + [pl.BlockSpec(memory_space=pltpu.SMEM)],
        out_specs=(hbm, pl.BlockSpec(memory_space=pltpu.VMEM)),
        scratch_shapes=[
            pltpu.VMEM((comp,) + inside, f32),
            pltpu.VMEM(rimmed, f32),
            pltpu.VMEM(inside, f32),
            pltpu.VMEM(inside, jnp.int32),
            pltpu.VMEM(inside, f32),
            pltpu.VMEM((6,) + inside, f32),
            pltpu.VMEM((NU, comp) + rimmed, f32),
            pltpu.VMEM((comp,) + inside, f32),
            pltpu.VMEM((4,) + face, f32),
            pltpu.VMEM((2,) + face, f32),
            pltpu.VMEM((NU, 4, comp) + face, f32),
            pltpu.VMEM((NU, 2, comp) + face, f32),
            pltpu.VMEM((4,) + face, f32),
            pltpu.VMEM((SUMS + 8, LOW), f32),
            pltpu.VMEM((n_gx, SUMS + 8, LOW), f32),
            pltpu.SemaphoreType.DMA((4, tiles_z)),
            pltpu.SemaphoreType.DMA((tiles_z,)),
            pltpu.SemaphoreType.DMA((NU + 1, 4)),
            pltpu.SemaphoreType.DMA((NU + 1, 4)),
            pltpu.SemaphoreType.DMA((n_gx,)),
            pltpu.SemaphoreType.DMA((n_gx,)),
        ],
        compiler_params=pltpu.CompilerParams(
            collective_id=0, has_side_effects=True, vmem_limit_bytes=56 * 2**20
        ),
    )(
        right_side.reshape((comp,) + whole),
        viscosity.reshape(whole),
        reaction.reshape(whole),
        agg_ids.reshape(whole),
        owner_map,
    )
    return velocity.reshape(right_side.shape), levels.transpose(0, 1, 3, 2, 4)


def solution(mesh):
    return jax.shard_map(
        functools.partial(shards, mesh.shape["gx"], mesh.shape["gy"]),
        mesh=mesh,
        in_specs=(
            P(None, "gx", "gy", None),
            P("gx", "gy", None),
            P("gx", "gy", None),
            P("gx", "gy", None),
            P("gx", "gy"),
        ),
        out_specs=(P(None, "gx", "gy", None), P("gx", "gy", None, None, None)),
        check_vma=False,
    )
```

```python
import functools

import jax
import jax.numpy as jnp
from jax import lax
from jax.experimental import pallas as pl
from jax.experimental.pallas import tpu as pltpu
from jax.sharding import PartitionSpec as P

COMP = 3
NAGG = 512
NU = 3
MERGES = 3
GROUP = 2**MERGES
LANES = 128
LOW = 64
HIGH = NAGG // LOW
PACKED = 2 * (COMP + 1) * HIGH
TILES = NAGG // LANES
SUMS = (COMP + 1) * TILES
MESH = pl.DeviceIdType.MESH


def kernel(
    dims,
    rs_hbm,
    visc_hbm,
    reac_hbm,
    ids_hbm,
    own_ref,
    vel_hbm,
    cor_ref,
    rs,
    visc,
    diag,
    ids,
    low_ids,
    high_ids,
    weight,
    vel,
    split,
    halo_visc,
    pack_visc,
    halo_vel,
    pack_vel,
    face_w,
    part,
    gathered,
    load_sem,
    store_sem,
    send_sem,
    recv_sem,
    all_send,
    all_recv,
):
    n_gx, n_gy, cx, cy, cz = dims
    rows = cx * cy
    tiles_z = cz // LANES
    gx, gy = lax.axis_index("gx"), lax.axis_index("gy")
    has = (gx > 0, gx < n_gx - 1, gy > 0, gy < n_gy - 1)
    targets = ((gx - 1, gy), (gx + 1, gy), (gx, gy - 1), (gx, gy + 1))

    def face(side, before=0):
        if side < 2:
            return pl.ds(before + (rows - cy if side else 0), cy)
        return pl.ds(before + (cy - 1 if side == 3 else 0), cx, stride=cy)

    block = pl.ds(cy, rows)
    sources = (visc_hbm, reac_hbm, ids_hbm, rs_hbm)
    loads = []
    for which, src in enumerate(sources):
        pieces = []
        for tile in range(tiles_z):
            lanes = pl.ds(tile * LANES, LANES)
            if which == 0:
                ends = src.at[:, lanes], visc.at[tile, block, :]
            elif which == 3:
                ends = src.at[:, :, lanes], rs.at[:, tile]
            else:
                ends = src.at[:, lanes], (diag if which == 1 else ids).at[tile]
            pieces.append(pltpu.make_async_copy(*ends, load_sem.at[which, tile]))
        loads.append(pieces)
    for pieces in loads:
        for piece in pieces:
            piece.start()

    def arrived(which):
        for piece in loads[which]:
            piece.wait()

    barrier = pltpu.get_barrier_semaphore()
    for step in range(1, n_gx):
        pl.semaphore_signal(
            barrier, inc=1, device_id=(lax.rem(gx + step, n_gx), gy), device_id_type=MESH
        )
    for side in (2, 3):

        @pl.when(has[side])
        def _():
            pl.semaphore_signal(barrier, inc=1, device_id=targets[side], device_id_type=MESH)

    empty = jnp.zeros((cy, LANES), jnp.float32)
    for tile in range(tiles_z):
        for rim in (0, rows + cy):
            visc[tile, rim : rim + cy, :] = empty
            for turn in range(NU):
                for comp in range(COMP):
                    vel[turn, comp, tile, rim : rim + cy, :] = empty

    arrived(0)
    for side in (2, 3):
        for tile in range(tiles_z):
            pack_visc[side - 2, tile] = visc[tile, face(side, cy), :]
    waits = (n_gx - 1) + has[2].astype(jnp.int32) + has[3].astype(jnp.int32)
    pl.semaphore_wait(barrier, waits)

    def face_copy(turn, side):
        other = side ^ 1
        if turn == 0:
            src = visc.at[:, face(side, cy), :] if side < 2 else pack_visc.at[side - 2]
            dst = halo_visc.at[other]
        else:
            src = (
                vel.at[turn - 1, :, :, face(side, cy), :]
                if side < 2
                else pack_vel.at[turn - 1, side - 2]
            )
            dst = halo_vel.at[turn - 1, other]
        return pltpu.make_async_remote_copy(
            src_ref=src,
            dst_ref=dst,
            send_sem=send_sem.at[turn, side],
            recv_sem=recv_sem.at[turn, other],
            device_id=targets[side],
            device_id_type=MESH,
        )

    def send_faces(turn):
        for side in range(4):

            @pl.when(has[side])
            def _():
                if turn and side >= 2:
                    for comp in range(COMP):
                        for tile in range(tiles_z):
                            pack_vel[turn - 1, side - 2, comp, tile] = vel[
                                turn - 1, comp, tile, face(side, cy), :
                            ]
                face_copy(turn, side).start()

    def with_faces(turn, work):
        for side in range(4):

            @pl.when(has[side])
            def _():
                face_copy(turn, side ^ 1).wait_recv()
                for tile in range(tiles_z):
                    work(side, tile)

    def drain(turn):
        for side in range(4):

            @pl.when(has[side])
            def _():
                face_copy(turn, side).wait_send()

    send_faces(0)
    shape = (cy, LANES)
    row_at = lax.broadcasted_iota(jnp.int32, shape, 0)
    lane_at = lax.broadcasted_iota(jnp.int32, shape, 1)
    no_high_y, no_low_y = row_at == cy - 1, row_at == 0
    last_lane, first_lane = lane_at == LANES - 1, lane_at == 0

    def plane(at, before=0):
        return pl.ds(pl.multiple_of(at * cy, cy) + before, cy)

    def beside_z(pieces, tile):
        here = pieces[tile]
        above = jnp.where(first_lane, pieces[(tile + 1) % tiles_z], here)
        under = jnp.where(last_lane, pieces[tile - 1], here)
        return pltpu.roll(above, LANES - 1, 1), pltpu.roll(under, 1, 1)

    def visc_beside(at, tile, pieces):
        high_z, low_z = beside_z(pieces, tile)
        if tile == tiles_z - 1:
            high_z = jnp.where(last_lane, 0.0, high_z)
        if tile == 0:
            low_z = jnp.where(first_lane, 0.0, low_z)
        return (
            visc[tile, plane(at, 2 * cy), :],
            visc[tile, plane(at), :],
            jnp.where(no_high_y, 0.0, visc[tile, plane(at, cy + 1), :]),
            jnp.where(no_low_y, 0.0, visc[tile, plane(at, cy - 1), :]),
            high_z,
            low_z,
        )

    arrived(1)

    @pl.loop(0, cx)
    def _(at):
        pieces = [visc[tile, plane(at, cy), :] for tile in range(tiles_z)]
        for tile in range(tiles_z):
            total = functools.reduce(jnp.add, visc_beside(at, tile, pieces))
            diag[tile, plane(at), :] = (
                diag[tile, plane(at), :] + 3.0 * pieces[tile] + 0.5 * total
            )

    arrived(2)

    @pl.loop(0, cx)
    def _(at):
        for tile in range(tiles_z):
            label = ids[tile, plane(at), :]
            low_ids[tile, plane(at), :] = (label & (LOW - 1)).astype(jnp.float32)
            high = lax.shift_right_logical(label, LOW.bit_length() - 1)
            high_ids[tile, plane(at), :] = high.astype(jnp.float32)

    def keep_parts(comp, tile, where, value):
        upper = value.astype(jnp.bfloat16).astype(jnp.float32)
        split[comp, tile, where, :] = upper
        split[COMP + 1 + comp, tile, where, :] = value - upper

    def add_visc(side, tile):
        diag[tile, face(side), :] = diag[tile, face(side), :] + 0.5 * halo_visc[side, tile]

    with_faces(0, add_visc)
    arrived(3)

    @pl.loop(0, cx)
    def _(at):
        pieces = [visc[tile, plane(at, cy), :] for tile in range(tiles_z)]
        for tile in range(tiles_z):
            here = pieces[tile]
            scale = 0.8 / diag[tile, plane(at), :]
            keep_parts(COMP, tile, plane(at), diag[tile, plane(at), :])
            for comp in range(COMP):
                vel[0, comp, tile, plane(at, cy), :] = scale * rs[comp, tile, plane(at), :]
            half = 0.5 * scale
            found = visc_beside(at, tile, pieces)
            drops = [None, None, no_high_y, no_low_y, None, None]
            if tile == tiles_z - 1:
                drops[4] = last_lane
            if tile == 0:
                drops[5] = first_lane
            for which, (other, drop) in enumerate(zip(found, drops)):
                ratio = half * (here + other)
                if drop is not None:
                    ratio = jnp.where(drop, 0.0, ratio)
                weight[which, tile, plane(at), :] = ratio

    send_faces(1)
    for side in range(4):

        @pl.when(has[side])
        def _():
            for tile in range(tiles_z):
                face_w[side, tile] = (
                    0.4
                    / diag[tile, face(side), :]
                    * (visc[tile, face(side, cy), :] + halo_visc[side, tile])
                )

    def from_beside(turn, at, write):
        pieces = [
            [vel[turn, comp, tile, plane(at, cy), :] for tile in range(tiles_z)]
            for comp in range(COMP)
        ]
        for tile in range(tiles_z):
            ratios = [weight[which, tile, plane(at), :] for which in range(6)]
            for comp in range(COMP):
                high_z, low_z = beside_z(pieces[comp], tile)
                total = ratios[0] * vel[turn, comp, tile, plane(at, 2 * cy), :]
                total += ratios[1] * vel[turn, comp, tile, plane(at), :]
                total += ratios[2] * vel[turn, comp, tile, plane(at, cy + 1), :]
                total += ratios[3] * vel[turn, comp, tile, plane(at, cy - 1), :]
                total += ratios[4] * high_z + ratios[5] * low_z
                write(comp, tile, pieces[comp][tile], total)

    for turn in range(1, NU):

        @pl.loop(0, cx)
        def _(at):
            def write(comp, tile, here, total):
                first = vel[0, comp, tile, plane(at, cy), :]
                vel[turn, comp, tile, plane(at, cy), :] = first + 0.2 * here + total

            from_beside(turn - 1, at, write)

        def add_vel(side, tile):
            ratio = face_w[side, tile]
            for comp in range(COMP):
                vel[turn, comp, tile, face(side, cy), :] = (
                    vel[turn, comp, tile, face(side, cy), :]
                    + ratio * halo_vel[turn - 1, side, comp, tile]
                )

        with_faces(turn, add_vel)
        send_faces(turn + 1)

    stores = [
        pltpu.make_async_copy(
            vel.at[NU - 1, :, tile, block, :],
            vel_hbm.at[:, :, pl.ds(tile * LANES, LANES)],
            store_sem.at[tile],
        )
        for tile in range(tiles_z)
    ]
    for store in stores:
        store.start()

    @pl.loop(0, cx)
    def _(at):
        def write(comp, tile, here, total):
            scale = 1.25 * diag[tile, plane(at), :]
            first = vel[0, comp, tile, plane(at, cy), :]
            keep_parts(comp, tile, plane(at), scale * (first - 0.8 * here + total))

        from_beside(NU - 1, at, write)

    high_at = lax.broadcasted_iota(jnp.int32, (16, LANES), 0) & (HIGH - 1)
    high_at = 2 * (high_at & (TILES - 1)) + lax.shift_right_logical(high_at, 2)
    high_at = high_at.astype(jnp.float32).astype(jnp.bfloat16)
    low_at = lax.broadcasted_iota(jnp.int32, (LOW, LANES), 0).astype(jnp.float32)
    low_at = low_at.astype(jnp.bfloat16)
    one, zero = jnp.ones((), jnp.bfloat16), jnp.zeros((), jnp.bfloat16)

    def add_row(total, row):
        tables, parts = [], []
        for tile in range(tiles_z):

            def spread(first, second):
                both = [jnp.broadcast_to(each, (HIGH, LANES)) for each in (first, second)]
                return jnp.concatenate(both, axis=0).astype(jnp.bfloat16)

            low = low_ids[tile, pl.ds(row, 1), :]
            low = jnp.concatenate([spread(low, low)] * (LOW // 16), axis=0)
            tables.append(jnp.where(low == low_at, one, zero))
            high = high_ids[tile, pl.ds(row, 1), :]
            is_high = spread(high, high) == high_at
            kept = []
            for at in range(0, 2 * (COMP + 1), 2):
                pair = spread(
                    split[at, tile, pl.ds(row, 1), :], split[at + 1, tile, pl.ds(row, 1), :]
                )
                kept.append(jnp.where(is_high, pair, zero))
            parts.append(jnp.concatenate(kept, axis=0))
        return total + lax.dot_general(
            jnp.concatenate(parts, axis=1),
            jnp.concatenate(tables, axis=1),
            (((1,), (1,)), ((), ())),
            preferred_element_type=jnp.float32,
        )

    def add_rows(total, start, within):
        def body(at, carried):
            for row in within:
                carried = add_row(carried, at * cy + row)
            return carried

        return lax.fori_loop(start[0], start[1], body, total)

    total = jnp.zeros((PACKED, LOW), jnp.float32)
    total = add_rows(total, (1, cx - 1), range(1, cy - 1))

    def add_res(side, tile):
        scale = 1.25 * diag[tile, face(side), :] * face_w[side, tile]
        for comp in range(COMP):
            value = split[comp, tile, face(side), :] + split[COMP + 1 + comp, tile, face(side), :]
            keep_parts(
                comp, tile, face(side), value + scale * halo_vel[NU - 1, side, comp, tile]
            )

    with_faces(NU, add_res)
    total = add_rows(total, (1, cx - 1), (0, cy - 1))
    total = add_rows(total, (0, 1), range(cy))
    total = add_rows(total, (cx - 1, cx), range(cy))

    total = total[: PACKED // 2] + total[PACKED // 2 :]
    for comp in range(COMP + 1):
        for half in range(2):
            start = comp * HIGH + half * TILES
            part[comp * TILES : (comp + 1) * TILES, half * LOW : (half + 1) * LOW] = total[
                start : start + TILES
            ]
    part[SUMS : SUMS + 8, :] = jnp.full((8, LANES), own_ref[0, 0], jnp.int32).astype(jnp.float32)

    def share(step):
        return pltpu.make_async_remote_copy(
            src_ref=part,
            dst_ref=gathered.at[step],
            send_sem=all_send.at[step],
            recv_sem=all_recv.at[step],
            device_id=(lax.rem(gx + step, n_gx), gy),
            device_id_type=MESH,
        )

    for step in range(1, n_gx):
        share(step).start()

    base = lax.div(gx, GROUP) * GROUP
    member = lax.broadcasted_iota(jnp.int32, (GROUP, LANES), 0)
    owner_of = (base + member).astype(jnp.float32)
    tiles = [jnp.zeros((GROUP, LANES), jnp.float32) for _ in range(SUMS)]
    for step in range(n_gx):
        if step:
            share(step).wait_recv()
        source = gathered.at[step] if step else part
        mine = source[SUMS : SUMS + 8, :] == owner_of
        for at in range(SUMS):
            row = jnp.broadcast_to(source[at : at + 1, :], (GROUP, LANES))
            tiles[at] = tiles[at] + jnp.where(mine, row, 0.0)
    owned = [
        jnp.concatenate(tiles[comp * TILES : (comp + 1) * TILES], axis=1) for comp in range(COMP + 1)
    ]
    coarse_res, coarse_diag = owned[:COMP], 1.0 + owned[COMP]
    lane = lax.broadcasted_iota(jnp.int32, (GROUP, NAGG), 1)
    member = lax.broadcasted_iota(jnp.int32, (GROUP, NAGG), 0)
    own_row = member == gx - base

    def partner(value, level):
        apart = 2**level
        odd = lax.rem(lax.div(member, apart), 2) == 1
        return jnp.where(
            odd, pltpu.roll(value, apart, 0), pltpu.roll(value, GROUP - apart, 0)
        )

    for level in range(MERGES + 1):
        coupling = 0.2 * jnp.minimum(coarse_diag, pltpu.roll(coarse_diag, NAGG - 1, 1))
        coupling = jnp.where(lane == NAGG - 1, 0.0, coupling)
        below = pltpu.roll(coupling, 1, 1)
        scale = 0.8 / coarse_diag

        def left(resid, vector):
            image = (
                coarse_diag * vector
                - coupling * pltpu.roll(vector, NAGG - 1, 1)
                - below * pltpu.roll(vector, 1, 1)
            )
            return resid - image

        merged = []
        for comp in range(COMP):
            resid = coarse_res[comp]
            error = scale * resid
            error = error + scale * left(resid, error)
            cor_ref[0, 0, comp, level : level + 1, :] = jnp.sum(
                jnp.where(own_row, error, 0.0), axis=0, keepdims=True
            )
            if level < MERGES:
                rest = left(resid, error)
                merged.append(rest + partner(rest, level))
        if level < MERGES:
            coarse_res = merged
            coarse_diag = coarse_diag + partner(coarse_diag, level)

    for turn in range(NU + 1):
        drain(turn)
    for step in range(1, n_gx):
        share(step).wait_send()
    for store in stores:
        store.wait()


def shards(n_gx, n_gy, right_side, viscosity, reaction, agg_ids, owner_map):
    comp, cx, cy, cz = right_side.shape
    rows = cx * cy
    whole = (rows, cz)
    tiles_z = cz // LANES
    inside = (tiles_z, rows, LANES)
    rimmed = (tiles_z, rows + 2 * cy, LANES)
    face = (tiles_z, cx, LANES)
    hbm = pl.BlockSpec(memory_space=pltpu.HBM)
    f32 = jnp.float32

    def stay(array):
        return pltpu.with_memory_space_constraint(array, pltpu.HBM)

    velocity, levels = pl.pallas_call(
        functools.partial(kernel, (n_gx, n_gy, cx, cy, cz)),
        out_shape=(
            jax.ShapeDtypeStruct((comp,) + whole, f32),
            jax.ShapeDtypeStruct((1, 1, comp, MERGES + 1, NAGG), f32),
        ),
        in_specs=[hbm] * 4 + [pl.BlockSpec(memory_space=pltpu.SMEM)],
        out_specs=(pl.BlockSpec(memory_space=pl.ANY), pl.BlockSpec(memory_space=pltpu.VMEM)),
        scratch_shapes=[
            pltpu.VMEM((comp,) + inside, f32),
            pltpu.VMEM(rimmed, f32),
            pltpu.VMEM(inside, f32),
            pltpu.VMEM(inside, jnp.int32),
            pltpu.VMEM(inside, f32),
            pltpu.VMEM(inside, f32),
            pltpu.VMEM((6,) + inside, f32),
            pltpu.VMEM((NU, comp) + rimmed, f32),
            pltpu.VMEM((2 * (comp + 1),) + inside, f32),
            pltpu.VMEM((4,) + face, f32),
            pltpu.VMEM((2,) + face, f32),
            pltpu.VMEM((NU, 4, comp) + face, f32),
            pltpu.VMEM((NU, 2, comp) + face, f32),
            pltpu.VMEM((4,) + face, f32),
            pltpu.VMEM((SUMS + 8, LANES), f32),
            pltpu.VMEM((n_gx, SUMS + 8, LANES), f32),
            pltpu.SemaphoreType.DMA((4, tiles_z)),
            pltpu.SemaphoreType.DMA((tiles_z,)),
            pltpu.SemaphoreType.DMA((NU + 1, 4)),
            pltpu.SemaphoreType.DMA((NU + 1, 4)),
            pltpu.SemaphoreType.DMA((n_gx,)),
            pltpu.SemaphoreType.DMA((n_gx,)),
        ],
        compiler_params=pltpu.CompilerParams(
            collective_id=0, has_side_effects=True, vmem_limit_bytes=30 * 2**20
        ),
    )(
        stay(right_side.reshape((comp,) + whole)),
        stay(viscosity.reshape(whole)),
        stay(reaction.reshape(whole)),
        stay(agg_ids.reshape(whole)),
        owner_map,
    )
    return velocity.reshape(right_side.shape), levels.transpose(0, 1, 3, 2, 4)


def solution(mesh):
    return jax.shard_map(
        functools.partial(shards, mesh.shape["gx"], mesh.shape["gy"]),
        mesh=mesh,
        in_specs=(
            P(None, "gx", "gy", None),
            P("gx", "gy", None),
            P("gx", "gy", None),
            P("gx", "gy", None),
            P("gx", "gy"),
        ),
        out_specs=(P(None, "gx", "gy", None), P("gx", "gy", None, None, None)),
        check_vma=False,
    )
```

```python
import functools

import jax
import jax.numpy as jnp
from jax import lax
from jax.experimental import pallas as pl
from jax.experimental.pallas import tpu as pltpu
from jax.sharding import PartitionSpec as P

COMP = 3
NAGG = 512
NU = 3
MERGES = 3
GROUP = 2**MERGES
LANES = 128
LOW = 64
HIGH = NAGG // LOW
PACKED = 2 * (COMP + 1) * HIGH
TILES = NAGG // LANES
SUMS = (COMP + 1) * TILES
MESH = pl.DeviceIdType.MESH


def kernel(
    dims,
    rs_hbm,
    visc_hbm,
    reac_hbm,
    ids_hbm,
    own_ref,
    vel_hbm,
    owned_ref,
    rs,
    visc,
    diag,
    ids,
    low_ids,
    high_ids,
    weight,
    vel,
    split,
    halo_visc,
    pack_visc,
    halo_vel,
    pack_vel,
    face_w,
    part,
    gathered,
    load_sem,
    store_sem,
    send_sem,
    recv_sem,
    all_send,
    all_recv,
):
    n_gx, n_gy, cx, cy, cz = dims
    rows = cx * cy
    tiles_z = cz // LANES
    gx, gy = lax.axis_index("gx"), lax.axis_index("gy")
    has = (gx > 0, gx < n_gx - 1, gy > 0, gy < n_gy - 1)
    targets = ((gx - 1, gy), (gx + 1, gy), (gx, gy - 1), (gx, gy + 1))

    def face(side, before=0):
        if side < 2:
            return pl.ds(before + (rows - cy if side else 0), cy)
        return pl.ds(before + (cy - 1 if side == 3 else 0), cx, stride=cy)

    block = pl.ds(cy, rows)
    sources = (visc_hbm, reac_hbm, ids_hbm, rs_hbm)
    loads = []
    for which, src in enumerate(sources):
        pieces = []
        for tile in range(tiles_z):
            lanes = pl.ds(tile * LANES, LANES)
            if which == 0:
                ends = src.at[:, lanes], visc.at[tile, block, :]
            elif which == 3:
                ends = src.at[:, :, lanes], rs.at[:, tile]
            else:
                ends = src.at[:, lanes], (diag if which == 1 else ids).at[tile]
            pieces.append(pltpu.make_async_copy(*ends, load_sem.at[which, tile]))
        loads.append(pieces)
    for pieces in loads:
        for piece in pieces:
            piece.start()

    def arrived(which):
        for piece in loads[which]:
            piece.wait()

    barrier = pltpu.get_barrier_semaphore()
    for step in range(1, n_gx):
        pl.semaphore_signal(
            barrier, inc=1, device_id=(lax.rem(gx + step, n_gx), gy), device_id_type=MESH
        )
    for side in (2, 3):

        @pl.when(has[side])
        def _():
            pl.semaphore_signal(barrier, inc=1, device_id=targets[side], device_id_type=MESH)

    empty = jnp.zeros((cy, LANES), jnp.float32)
    for tile in range(tiles_z):
        for rim in (0, rows + cy):
            visc[tile, rim : rim + cy, :] = empty
            for turn in range(NU):
                for comp in range(COMP):
                    vel[turn, comp, tile, rim : rim + cy, :] = empty

    arrived(0)
    for side in (2, 3):
        for tile in range(tiles_z):
            pack_visc[side - 2, tile] = visc[tile, face(side, cy), :]
    waits = (n_gx - 1) + has[2].astype(jnp.int32) + has[3].astype(jnp.int32)
    pl.semaphore_wait(barrier, waits)

    def face_copy(turn, side, comp=0):
        other = side ^ 1
        if turn == 0:
            src = visc.at[:, face(side, cy), :] if side < 2 else pack_visc.at[side - 2]
            dst = halo_visc.at[other]
        else:
            src = (
                vel.at[turn - 1, comp, :, face(side, cy), :]
                if side < 2
                else pack_vel.at[turn - 1, side - 2, comp]
            )
            dst = halo_vel.at[turn - 1, other, comp]
        return pltpu.make_async_remote_copy(
            src_ref=src,
            dst_ref=dst,
            send_sem=send_sem.at[turn, side, comp],
            recv_sem=recv_sem.at[turn, other, comp],
            device_id=targets[side],
            device_id_type=MESH,
        )

    def send_faces(turn, comp=0, sides=(2, 3, 0, 1), pack=True):
        for side in sides:

            @pl.when(has[side])
            def _():
                if turn and side >= 2 and pack:
                    for tile in range(tiles_z):
                        pack_vel[turn - 1, side - 2, comp, tile] = vel[
                            turn - 1, comp, tile, face(side, cy), :
                        ]
                face_copy(turn, side, comp).start()

    def with_faces(turn, comp, work):
        for side in range(4):

            @pl.when(has[side])
            def _():
                face_copy(turn, side ^ 1, comp).wait_recv()
                for tile in range(tiles_z):
                    work(side, tile)

    def drain(turn, comp=0):
        for side in range(4):

            @pl.when(has[side])
            def _():
                face_copy(turn, side, comp).wait_send()

    send_faces(0)
    shape = (cy, LANES)
    row_at = lax.broadcasted_iota(jnp.int32, shape, 0)
    lane_at = lax.broadcasted_iota(jnp.int32, shape, 1)
    no_high_y, no_low_y = row_at == cy - 1, row_at == 0
    last_lane, first_lane = lane_at == LANES - 1, lane_at == 0

    def plane(at, before=0):
        start = at * cy if isinstance(at, int) else pl.multiple_of(at * cy, cy)
        return pl.ds(start + before, cy)

    def beside_z(pieces, tile):
        here = pieces[tile]
        above = jnp.where(first_lane, pieces[(tile + 1) % tiles_z], here)
        under = jnp.where(last_lane, pieces[tile - 1], here)
        return pltpu.roll(above, LANES - 1, 1), pltpu.roll(under, 1, 1)

    def visc_beside(at, tile, pieces):
        high_z, low_z = beside_z(pieces, tile)
        if tile == tiles_z - 1:
            high_z = jnp.where(last_lane, 0.0, high_z)
        if tile == 0:
            low_z = jnp.where(first_lane, 0.0, low_z)
        return (
            visc[tile, plane(at, 2 * cy), :],
            visc[tile, plane(at), :],
            jnp.where(no_high_y, 0.0, visc[tile, plane(at, cy + 1), :]),
            jnp.where(no_low_y, 0.0, visc[tile, plane(at, cy - 1), :]),
            high_z,
            low_z,
        )

    arrived(1)

    @pl.loop(0, cx)
    def _(at):
        pieces = [visc[tile, plane(at, cy), :] for tile in range(tiles_z)]
        for tile in range(tiles_z):
            total = functools.reduce(jnp.add, visc_beside(at, tile, pieces))
            diag[tile, plane(at), :] = (
                diag[tile, plane(at), :] + 3.0 * pieces[tile] + 0.5 * total
            )

    arrived(2)

    @pl.loop(0, cx)
    def _(at):
        for tile in range(tiles_z):
            label = ids[tile, plane(at), :]
            low_ids[tile, plane(at), :] = (label & (LOW - 1)).astype(jnp.float32)
            high = lax.shift_right_logical(label, LOW.bit_length() - 1)
            high_ids[tile, plane(at), :] = high.astype(jnp.float32)

    def keep_parts(comp, tile, where, value):
        upper = value.astype(jnp.bfloat16).astype(jnp.float32)
        split[comp, tile, where, :] = upper
        split[COMP + 1 + comp, tile, where, :] = value - upper

    def add_visc(side, tile):
        diag[tile, face(side), :] = diag[tile, face(side), :] + 0.5 * halo_visc[side, tile]

    with_faces(0, 0, add_visc)
    arrived(3)

    for side in (2, 3):

        @pl.when(has[side])
        def _():
            for tile in range(tiles_z):
                scale = 0.8 / diag[tile, face(side), :]
                for comp in range(COMP):
                    pack_vel[0, side - 2, comp, tile] = scale * rs[comp, tile, face(side), :]

    for comp in range(COMP):
        send_faces(1, comp, (2, 3), False)

    def scale_plane(at):
        pieces = [visc[tile, plane(at, cy), :] for tile in range(tiles_z)]
        for tile in range(tiles_z):
            here = pieces[tile]
            scale = 0.8 / diag[tile, plane(at), :]
            keep_parts(COMP, tile, plane(at), diag[tile, plane(at), :])
            for comp in range(COMP):
                vel[0, comp, tile, plane(at, cy), :] = scale * rs[comp, tile, plane(at), :]
            half = 0.5 * scale
            found = visc_beside(at, tile, pieces)
            drops = [None, None, no_high_y, no_low_y, None, None]
            if tile == tiles_z - 1:
                drops[4] = last_lane
            if tile == 0:
                drops[5] = first_lane
            for which, (other, drop) in enumerate(zip(found, drops)):
                ratio = half * (here + other)
                if drop is not None:
                    ratio = jnp.where(drop, 0.0, ratio)
                weight[which, tile, plane(at), :] = ratio

    scale_plane(0)
    scale_plane(cx - 1)
    for comp in range(COMP):
        send_faces(1, comp, (0, 1))
    pl.loop(1, cx - 1)(scale_plane)
    for side in range(4):

        @pl.when(has[side])
        def _():
            for tile in range(tiles_z):
                face_w[side, tile] = (
                    0.4
                    / diag[tile, face(side), :]
                    * (visc[tile, face(side, cy), :] + halo_visc[side, tile])
                )

    def from_beside(turn, at, write, comps):
        pieces = {
            comp: [vel[turn, comp, tile, plane(at, cy), :] for tile in range(tiles_z)]
            for comp in comps
        }
        for tile in range(tiles_z):
            ratios = [weight[which, tile, plane(at), :] for which in range(6)]
            for comp in comps:
                high_z, low_z = beside_z(pieces[comp], tile)
                total = ratios[0] * vel[turn, comp, tile, plane(at, 2 * cy), :]
                total += ratios[1] * vel[turn, comp, tile, plane(at), :]
                total += ratios[2] * vel[turn, comp, tile, plane(at, cy + 1), :]
                total += ratios[3] * vel[turn, comp, tile, plane(at, cy - 1), :]
                total += ratios[4] * high_z + ratios[5] * low_z
                write(comp, tile, pieces[comp][tile], total)

    def sweep(turn, comp):
        @pl.loop(0, cx)
        def _(at):
            def write(comp, tile, here, total):
                first = vel[0, comp, tile, plane(at, cy), :]
                vel[turn, comp, tile, plane(at, cy), :] = first + 0.2 * here + total

            from_beside(turn - 1, at, write, (comp,))

        def add_vel(side, tile):
            vel[turn, comp, tile, face(side, cy), :] = (
                vel[turn, comp, tile, face(side, cy), :]
                + face_w[side, tile] * halo_vel[turn - 1, side, comp, tile]
            )

        with_faces(turn, comp, add_vel)
        send_faces(turn + 1, comp)

    for turn in range(1, NU):
        for comp in range(COMP):
            sweep(turn, comp)

    stores = [
        pltpu.make_async_copy(
            vel.at[NU - 1, :, tile, block, :],
            vel_hbm.at[:, :, pl.ds(tile * LANES, LANES)],
            store_sem.at[tile],
        )
        for tile in range(tiles_z)
    ]
    for store in stores:
        store.start()

    @pl.loop(0, cx)
    def _(at):
        def write(comp, tile, here, total):
            scale = 1.25 * diag[tile, plane(at), :]
            first = vel[0, comp, tile, plane(at, cy), :]
            keep_parts(comp, tile, plane(at), scale * (first - 0.8 * here + total))

        from_beside(NU - 1, at, write, range(COMP))

    high_at = lax.broadcasted_iota(jnp.int32, (16, LANES), 0) & (HIGH - 1)
    high_at = 2 * (high_at & (TILES - 1)) + lax.shift_right_logical(high_at, 2)
    high_at = high_at.astype(jnp.float32).astype(jnp.bfloat16)
    low_at = lax.broadcasted_iota(jnp.int32, (LOW, LANES), 0).astype(jnp.float32)
    low_at = low_at.astype(jnp.bfloat16)
    one, zero = jnp.ones((), jnp.bfloat16), jnp.zeros((), jnp.bfloat16)

    def add_row(total, row):
        tables, parts = [], []
        for tile in range(tiles_z):

            def spread(first, second):
                both = [jnp.broadcast_to(each, (HIGH, LANES)) for each in (first, second)]
                return jnp.concatenate(both, axis=0).astype(jnp.bfloat16)

            low = low_ids[tile, pl.ds(row, 1), :]
            low = jnp.concatenate([spread(low, low)] * (LOW // 16), axis=0)
            tables.append(jnp.where(low == low_at, one, zero))
            high = high_ids[tile, pl.ds(row, 1), :]
            is_high = spread(high, high) == high_at
            kept = []
            for at in range(0, 2 * (COMP + 1), 2):
                pair = spread(
                    split[at, tile, pl.ds(row, 1), :], split[at + 1, tile, pl.ds(row, 1), :]
                )
                kept.append(jnp.where(is_high, pair, zero))
            parts.append(jnp.concatenate(kept, axis=0))
        return total + lax.dot_general(
            jnp.concatenate(parts, axis=1),
            jnp.concatenate(tables, axis=1),
            (((1,), (1,)), ((), ())),
            preferred_element_type=jnp.float32,
        )

    def add_rows(total, start, within):
        def body(at, carried):
            for row in within:
                carried = add_row(carried, at * cy + row)
            return carried

        return lax.fori_loop(start[0], start[1], body, total)

    total = jnp.zeros((PACKED, LOW), jnp.float32)
    total = add_rows(total, (1, cx - 1), range(1, cy - 1))

    for comp in range(COMP):

        def add_res(side, tile):
            scale = 1.25 * diag[tile, face(side), :] * face_w[side, tile]
            value = split[comp, tile, face(side), :] + split[COMP + 1 + comp, tile, face(side), :]
            keep_parts(
                comp, tile, face(side), value + scale * halo_vel[NU - 1, side, comp, tile]
            )

        with_faces(NU, comp, add_res)

    total = add_rows(total, (1, cx - 1), (0, cy - 1))
    total = add_rows(total, (0, 1), range(cy))
    total = add_rows(total, (cx - 1, cx), range(cy))

    total = total[: PACKED // 2] + total[PACKED // 2 :]
    for comp in range(COMP + 1):
        for half in range(2):
            start = comp * HIGH + half * TILES
            part[comp * TILES : (comp + 1) * TILES, half * LOW : (half + 1) * LOW] = total[
                start : start + TILES
            ]
    part[SUMS : SUMS + 8, :] = jnp.full((8, LANES), own_ref[0, 0], jnp.int32).astype(jnp.float32)

    def share(step):
        return pltpu.make_async_remote_copy(
            src_ref=part,
            dst_ref=gathered.at[step],
            send_sem=all_send.at[step],
            recv_sem=all_recv.at[step],
            device_id=(lax.rem(gx + step, n_gx), gy),
            device_id_type=MESH,
        )

    for step in range(1, n_gx):
        share(step).start()

    base = lax.div(gx, GROUP) * GROUP
    member = lax.broadcasted_iota(jnp.int32, (GROUP, LANES), 0)
    owner_of = (base + member).astype(jnp.float32)
    tiles = [jnp.zeros((GROUP, LANES), jnp.float32) for _ in range(SUMS)]
    for step in range(n_gx):
        if step:
            share(step).wait_recv()
        source = gathered.at[step] if step else part
        mine = source[SUMS : SUMS + 8, :] == owner_of
        for at in range(SUMS):
            row = jnp.broadcast_to(source[at : at + 1, :], (GROUP, LANES))
            tiles[at] = tiles[at] + jnp.where(mine, row, 0.0)
    for at in range(SUMS):
        owned_ref[at] = tiles[at]
    drain(0)
    for turn in range(1, NU + 1):
        for comp in range(COMP):
            drain(turn, comp)
    for step in range(1, n_gx):
        share(step).wait_send()
    for store in stores:
        store.wait()


def coarse_kernel(vel_in, owned_ref, vel_out, cor_ref, sem):
    copies = [
        pltpu.make_async_copy(vel_in.at[comp], vel_out.at[comp], sem.at[comp])
        for comp in range(COMP)
    ]
    for copy in copies:
        copy.start()
    gx = lax.axis_index("gx")
    base = lax.div(gx, GROUP) * GROUP
    owned = [
        jnp.concatenate([owned_ref[comp * TILES + at] for at in range(TILES)], axis=1)
        for comp in range(COMP + 1)
    ]
    coarse_res, coarse_diag = owned[:COMP], 1.0 + owned[COMP]
    lane = lax.broadcasted_iota(jnp.int32, (GROUP, NAGG), 1)
    member = lax.broadcasted_iota(jnp.int32, (GROUP, NAGG), 0)
    own_row = member == gx - base

    def partner(value, level):
        apart = 2**level
        odd = lax.rem(lax.div(member, apart), 2) == 1
        return jnp.where(
            odd, pltpu.roll(value, apart, 0), pltpu.roll(value, GROUP - apart, 0)
        )

    for level in range(MERGES + 1):
        coupling = 0.2 * jnp.minimum(coarse_diag, pltpu.roll(coarse_diag, NAGG - 1, 1))
        coupling = jnp.where(lane == NAGG - 1, 0.0, coupling)
        below = pltpu.roll(coupling, 1, 1)
        scale = 0.8 / coarse_diag

        def left(resid, vector):
            image = (
                coarse_diag * vector
                - coupling * pltpu.roll(vector, NAGG - 1, 1)
                - below * pltpu.roll(vector, 1, 1)
            )
            return resid - image

        merged = []
        for comp in range(COMP):
            resid = coarse_res[comp]
            error = scale * resid
            error = error + scale * left(resid, error)
            cor_ref[0, 0, comp, level : level + 1, :] = jnp.sum(
                jnp.where(own_row, error, 0.0), axis=0, keepdims=True
            )
            if level < MERGES:
                rest = left(resid, error)
                merged.append(rest + partner(rest, level))
        if level < MERGES:
            coarse_res = merged
            coarse_diag = coarse_diag + partner(coarse_diag, level)

    for copy in copies:
        copy.wait()


def shards(n_gx, n_gy, right_side, viscosity, reaction, agg_ids, owner_map):
    comp, cx, cy, cz = right_side.shape
    rows = cx * cy
    whole = (rows, cz)
    tiles_z = cz // LANES
    inside = (tiles_z, rows, LANES)
    rimmed = (tiles_z, rows + 2 * cy, LANES)
    face = (tiles_z, cx, LANES)
    hbm = pl.BlockSpec(memory_space=pltpu.HBM)
    f32 = jnp.float32

    def stay(array):
        return pltpu.with_memory_space_constraint(array, pltpu.HBM)

    velocity, owned = pl.pallas_call(
        functools.partial(kernel, (n_gx, n_gy, cx, cy, cz)),
        out_shape=(
            jax.ShapeDtypeStruct((comp,) + whole, f32),
            jax.ShapeDtypeStruct((SUMS, GROUP, LANES), f32),
        ),
        in_specs=[hbm] * 4 + [pl.BlockSpec(memory_space=pltpu.SMEM)],
        out_specs=(pl.BlockSpec(memory_space=pl.ANY), pl.BlockSpec(memory_space=pltpu.VMEM)),
        scratch_shapes=[
            pltpu.VMEM((comp,) + inside, f32),
            pltpu.VMEM(rimmed, f32),
            pltpu.VMEM(inside, f32),
            pltpu.VMEM(inside, jnp.int32),
            pltpu.VMEM(inside, f32),
            pltpu.VMEM(inside, f32),
            pltpu.VMEM((6,) + inside, f32),
            pltpu.VMEM((NU, comp) + rimmed, f32),
            pltpu.VMEM((2 * (comp + 1),) + inside, f32),
            pltpu.VMEM((4,) + face, f32),
            pltpu.VMEM((2,) + face, f32),
            pltpu.VMEM((NU, 4, comp) + face, f32),
            pltpu.VMEM((NU, 2, comp) + face, f32),
            pltpu.VMEM((4,) + face, f32),
            pltpu.VMEM((SUMS + 8, LANES), f32),
            pltpu.VMEM((n_gx, SUMS + 8, LANES), f32),
            pltpu.SemaphoreType.DMA((4, tiles_z)),
            pltpu.SemaphoreType.DMA((tiles_z,)),
            pltpu.SemaphoreType.DMA((NU + 1, 4, COMP)),
            pltpu.SemaphoreType.DMA((NU + 1, 4, COMP)),
            pltpu.SemaphoreType.DMA((n_gx,)),
            pltpu.SemaphoreType.DMA((n_gx,)),
        ],
        compiler_params=pltpu.CompilerParams(
            collective_id=0, has_side_effects=True, vmem_limit_bytes=30 * 2**20
        ),
    )(
        stay(right_side.reshape((comp,) + whole)),
        stay(viscosity.reshape(whole)),
        stay(reaction.reshape(whole)),
        stay(agg_ids.reshape(whole)),
        owner_map,
    )
    velocity, levels = pl.pallas_call(
        coarse_kernel,
        out_shape=(
            jax.ShapeDtypeStruct((comp,) + whole, f32),
            jax.ShapeDtypeStruct((1, 1, comp, MERGES + 1, NAGG), f32),
        ),
        in_specs=[pl.BlockSpec(memory_space=pl.ANY), pl.BlockSpec(memory_space=pltpu.VMEM)],
        out_specs=(hbm, pl.BlockSpec(memory_space=pltpu.VMEM)),
        scratch_shapes=[pltpu.SemaphoreType.DMA((COMP,))],
        compiler_params=pltpu.CompilerParams(vmem_limit_bytes=8 * 2**20),
    )(velocity, owned)
    return velocity.reshape(right_side.shape), levels.transpose(0, 1, 3, 2, 4)


def solution(mesh):
    return jax.shard_map(
        functools.partial(shards, mesh.shape["gx"], mesh.shape["gy"]),
        mesh=mesh,
        in_specs=(
            P(None, "gx", "gy", None),
            P("gx", "gy", None),
            P("gx", "gy", None),
            P("gx", "gy", None),
            P("gx", "gy"),
        ),
        out_specs=(P(None, "gx", "gy", None), P("gx", "gy", None, None, None)),
        check_vma=False,
    )
```

```python
import functools

import jax
import jax.numpy as jnp
from jax import lax
from jax.experimental import pallas as pl
from jax.experimental.pallas import tpu as pltpu
from jax.sharding import PartitionSpec as P

COMP = 3
NAGG = 512
NU = 3
MERGES = 3
GROUP = 2**MERGES
LANES = 128
LOW = 64
HIGH = NAGG // LOW
PACKED = 2 * (COMP + 1) * HIGH
TILES = NAGG // LANES
SUMS = (COMP + 1) * TILES
MESH = pl.DeviceIdType.MESH


def kernel(
    dims,
    rs_hbm,
    visc_hbm,
    reac_hbm,
    ids_hbm,
    own_ref,
    vel_hbm,
    owned_ref,
    rs,
    visc,
    reac,
    diag,
    ids,
    low_ids,
    high_ids,
    weight,
    vel,
    split,
    halo_visc,
    pack_visc,
    halo_vel,
    pack_vel,
    face_w,
    part,
    gathered,
    load_sem,
    store_sem,
    send_sem,
    recv_sem,
    all_send,
    all_recv,
):
    n_gx, n_gy, cx, cy, cz = dims
    rows = cx * cy
    tiles_z = cz // LANES
    gx, gy = lax.axis_index("gx"), lax.axis_index("gy")
    has = (gx > 0, gx < n_gx - 1, gy > 0, gy < n_gy - 1)
    targets = ((gx - 1, gy), (gx + 1, gy), (gx, gy - 1), (gx, gy + 1))

    def face(side, before=0):
        if side < 2:
            return pl.ds(before + (rows - cy if side else 0), cy)
        return pl.ds(before + (cy - 1 if side == 3 else 0), cx, stride=cy)

    block = pl.ds(cy, rows)
    sources = (visc_hbm, reac_hbm, ids_hbm, rs_hbm)
    loads = []
    for which, src in enumerate(sources):
        pieces = []
        for tile in range(tiles_z):
            lanes = pl.ds(tile * LANES, LANES)
            if which == 0:
                ends = src.at[:, lanes], visc.at[tile, block, :]
            elif which == 3:
                ends = src.at[:, :, lanes], rs.at[:, tile]
            else:
                ends = src.at[:, lanes], (reac if which == 1 else ids).at[tile]
            pieces.append(pltpu.make_async_copy(*ends, load_sem.at[which, tile]))
        loads.append(pieces)
    for pieces in loads:
        for piece in pieces:
            piece.start()

    def arrived(which):
        for piece in loads[which]:
            piece.wait()

    barrier = pltpu.get_barrier_semaphore()
    for step in range(1, n_gx):
        pl.semaphore_signal(
            barrier, inc=1, device_id=(lax.rem(gx + step, n_gx), gy), device_id_type=MESH
        )
    for side in (2, 3):

        @pl.when(has[side])
        def _():
            pl.semaphore_signal(barrier, inc=1, device_id=targets[side], device_id_type=MESH)

    empty = jnp.zeros((cy, LANES), jnp.float32)
    for tile in range(tiles_z):
        for rim in (0, rows + cy):
            visc[tile, rim : rim + cy, :] = empty
            for turn in range(NU):
                for comp in range(COMP):
                    vel[turn][comp, tile, rim : rim + cy, :] = empty

    arrived(0)
    for side in (2, 3):
        for tile in range(tiles_z):
            pack_visc[side - 2, tile] = visc[tile, face(side, cy), :]
    waits = (n_gx - 1) + has[2].astype(jnp.int32) + has[3].astype(jnp.int32)
    pl.semaphore_wait(barrier, waits)

    def face_copy(turn, side, comp=0):
        other = side ^ 1
        if turn == 0:
            src = visc.at[:, face(side, cy), :] if side < 2 else pack_visc.at[side - 2]
            dst = halo_visc.at[other]
        else:
            src = (
                vel[turn - 1].at[comp, :, face(side, cy), :]
                if side < 2
                else pack_vel.at[turn - 1, side - 2, comp]
            )
            dst = halo_vel.at[turn - 1, other, comp]
        return pltpu.make_async_remote_copy(
            src_ref=src,
            dst_ref=dst,
            send_sem=send_sem.at[turn, side, comp],
            recv_sem=recv_sem.at[turn, other, comp],
            device_id=targets[side],
            device_id_type=MESH,
        )

    def send_faces(turn, comp=0, sides=(2, 3, 0, 1), pack=True):
        for side in sides:

            @pl.when(has[side])
            def _():
                if turn and side >= 2 and pack:
                    for tile in range(tiles_z):
                        pack_vel[turn - 1, side - 2, comp, tile] = vel[turn - 1][comp, tile, face(side, cy), :
                        ]
                face_copy(turn, side, comp).start()

    def with_faces(turn, comp, work):
        for side in range(4):

            @pl.when(has[side])
            def _():
                face_copy(turn, side ^ 1, comp).wait_recv()
                stores = [work(side, tile) for tile in range(tiles_z)]
                for store in stores:
                    store()

    def drain(turn, comp=0):
        for side in range(4):

            @pl.when(has[side])
            def _():
                face_copy(turn, side, comp).wait_send()

    send_faces(0)
    shape = (cy, LANES)
    row_at = lax.broadcasted_iota(jnp.int32, shape, 0)
    lane_at = lax.broadcasted_iota(jnp.int32, shape, 1)
    no_high_y, no_low_y = row_at == cy - 1, row_at == 0
    last_lane, first_lane = lane_at == LANES - 1, lane_at == 0

    def plane(at, before=0):
        start = at * cy if isinstance(at, int) else pl.multiple_of(at * cy, cy)
        return pl.ds(start + before, cy)

    def beside_z(pieces, tile):
        here = pieces[tile]
        above = jnp.where(first_lane, pieces[(tile + 1) % tiles_z], here)
        under = jnp.where(last_lane, pieces[tile - 1], here)
        return pltpu.roll(above, LANES - 1, 1), pltpu.roll(under, 1, 1)

    def visc_beside(at, tile, pieces):
        high_z, low_z = beside_z(pieces, tile)
        if tile == tiles_z - 1:
            high_z = jnp.where(last_lane, 0.0, high_z)
        if tile == 0:
            low_z = jnp.where(first_lane, 0.0, low_z)
        return (
            visc[tile, plane(at, 2 * cy), :],
            visc[tile, plane(at), :],
            jnp.where(no_high_y, 0.0, visc[tile, plane(at, cy + 1), :]),
            jnp.where(no_low_y, 0.0, visc[tile, plane(at, cy - 1), :]),
            high_z,
            low_z,
        )

    def planes(start, end, together):
        def each(work):
            together_now = together
            while (end - start) % together_now:
                together_now -= 1

            @pl.loop(0, (end - start) // together_now)
            def _(turn):
                for inner in range(together_now):
                    work(start + turn * together_now + inner)

        return each

    arrived(1)

    @planes(0, cx, 4)
    def _(at):
        pieces = [visc[tile, plane(at, cy), :] for tile in range(tiles_z)]
        for tile in range(tiles_z):
            total = functools.reduce(jnp.add, visc_beside(at, tile, pieces))
            diag[tile, plane(at), :] = (
                reac[tile, plane(at), :] + 3.0 * pieces[tile] + 0.5 * total
            )

    arrived(2)

    @planes(0, cx, 4)
    def _(at):
        for tile in range(tiles_z):
            label = ids[tile, plane(at), :]
            low_ids[tile, plane(at), :] = (label & (LOW - 1)).astype(jnp.float32)
            high = lax.shift_right_logical(label, LOW.bit_length() - 1)
            high_ids[tile, plane(at), :] = high.astype(jnp.float32)

    def keep_parts(comp, tile, where, value):
        upper = value.astype(jnp.bfloat16).astype(jnp.float32)
        split[comp, tile, where, :] = upper
        split[COMP + 1 + comp, tile, where, :] = value - upper

    def add_visc(side, tile):
        value = diag[tile, face(side), :] + 0.5 * halo_visc[side, tile]

        def store():
            diag[tile, face(side), :] = value

        return store

    with_faces(0, 0, add_visc)
    arrived(3)

    for side in (2, 3):

        @pl.when(has[side])
        def _():
            for tile in range(tiles_z):
                scale = 0.8 / diag[tile, face(side), :]
                for comp in range(COMP):
                    pack_vel[0, side - 2, comp, tile] = scale * rs[comp, tile, face(side), :]

    for comp in range(COMP):
        send_faces(1, comp, (2, 3), False)

    def scale_plane(at):
        pieces = [visc[tile, plane(at, cy), :] for tile in range(tiles_z)]
        for tile in range(tiles_z):
            here = pieces[tile]
            scale = 0.8 / diag[tile, plane(at), :]
            keep_parts(COMP, tile, plane(at), diag[tile, plane(at), :])
            for comp in range(COMP):
                vel[0][comp, tile, plane(at, cy), :] = scale * rs[comp, tile, plane(at), :]
            half = 0.5 * scale
            found = visc_beside(at, tile, pieces)
            drops = [None, None, no_high_y, no_low_y, None, None]
            if tile == tiles_z - 1:
                drops[4] = last_lane
            if tile == 0:
                drops[5] = first_lane
            for which, (other, drop) in enumerate(zip(found, drops)):
                ratio = half * (here + other)
                if drop is not None:
                    ratio = jnp.where(drop, 0.0, ratio)
                weight[which, tile, plane(at), :] = ratio

    scale_plane(0)
    scale_plane(cx - 1)
    for comp in range(COMP):
        send_faces(1, comp, (0, 1))
    planes(1, cx - 1, 2)(scale_plane)
    for side in range(4):

        @pl.when(has[side])
        def _():
            for tile in range(tiles_z):
                face_w[side, tile] = (
                    0.4
                    / diag[tile, face(side), :]
                    * (visc[tile, face(side, cy), :] + halo_visc[side, tile])
                )

    def from_beside(turn, at, write, comps):
        pieces = {
            comp: [vel[turn][comp, tile, plane(at, cy), :] for tile in range(tiles_z)]
            for comp in comps
        }
        for tile in range(tiles_z):
            ratios = [weight[which, tile, plane(at), :] for which in range(6)]
            for comp in comps:
                high_z, low_z = beside_z(pieces[comp], tile)
                total = ratios[0] * vel[turn][comp, tile, plane(at, 2 * cy), :]
                total += ratios[1] * vel[turn][comp, tile, plane(at), :]
                total += ratios[2] * vel[turn][comp, tile, plane(at, cy + 1), :]
                total += ratios[3] * vel[turn][comp, tile, plane(at, cy - 1), :]
                total += ratios[4] * high_z + ratios[5] * low_z
                write(comp, tile, pieces[comp][tile], total)

    def sweep(turn, comp):
        @planes(0, cx, 4)
        def _(at):
            def write(comp, tile, here, total):
                first = vel[0][comp, tile, plane(at, cy), :]
                vel[turn][comp, tile, plane(at, cy), :] = first + 0.2 * here + total

            from_beside(turn - 1, at, write, (comp,))

        def add_vel(side, tile):
            value = (
                vel[turn][comp, tile, face(side, cy), :]
                + face_w[side, tile] * halo_vel[turn - 1, side, comp, tile]
            )

            def store():
                vel[turn][comp, tile, face(side, cy), :] = value

            return store

        with_faces(turn, comp, add_vel)
        send_faces(turn + 1, comp)

    for turn in range(1, NU):
        for comp in range(COMP):
            sweep(turn, comp)

    stores = [
        pltpu.make_async_copy(
            vel[NU - 1].at[:, tile, block, :],
            vel_hbm.at[:, :, pl.ds(tile * LANES, LANES)],
            store_sem.at[tile],
        )
        for tile in range(tiles_z)
    ]
    for store in stores:
        store.start()

    @planes(0, cx, 2)
    def _(at):
        def write(comp, tile, here, total):
            scale = 1.25 * diag[tile, plane(at), :]
            first = vel[0][comp, tile, plane(at, cy), :]
            keep_parts(comp, tile, plane(at), scale * (first - 0.8 * here + total))

        from_beside(NU - 1, at, write, range(COMP))

    high_at = lax.broadcasted_iota(jnp.int32, (16, LANES), 0) & (HIGH - 1)
    high_at = 2 * (high_at & (TILES - 1)) + lax.shift_right_logical(high_at, 2)
    high_at = high_at.astype(jnp.float32).astype(jnp.bfloat16)
    low_at = lax.broadcasted_iota(jnp.int32, (LOW, LANES), 0).astype(jnp.float32)
    low_at = low_at.astype(jnp.bfloat16)
    one, zero = jnp.ones((), jnp.bfloat16), jnp.zeros((), jnp.bfloat16)

    def add_row(total, row):
        tables, parts = [], []
        for tile in range(tiles_z):

            def spread(first, second):
                both = [jnp.broadcast_to(each, (HIGH, LANES)) for each in (first, second)]
                return jnp.concatenate(both, axis=0).astype(jnp.bfloat16)

            low = low_ids[tile, pl.ds(row, 1), :]
            low = jnp.concatenate([spread(low, low)] * (LOW // 16), axis=0)
            tables.append(jnp.where(low == low_at, one, zero))
            high = high_ids[tile, pl.ds(row, 1), :]
            is_high = spread(high, high) == high_at
            kept = []
            for at in range(0, 2 * (COMP + 1), 2):
                pair = spread(
                    split[at, tile, pl.ds(row, 1), :], split[at + 1, tile, pl.ds(row, 1), :]
                )
                kept.append(jnp.where(is_high, pair, zero))
            parts.append(jnp.concatenate(kept, axis=0))
        return total + lax.dot_general(
            jnp.concatenate(parts, axis=1),
            jnp.concatenate(tables, axis=1),
            (((1,), (1,)), ((), ())),
            preferred_element_type=jnp.float32,
        )

    def add_rows(total, start, end, within, together):
        while (end - start) % together:
            together -= 1

        def body(turn, carried):
            for inner in range(together):
                for row in within:
                    at = start + turn * together + inner
                    carried = add_row(carried, at * cy + row)
            return carried

        return lax.fori_loop(0, (end - start) // together, body, total)

    total = jnp.zeros((PACKED, LOW), jnp.float32)
    total = add_rows(total, 1, cx - 1, range(1, cy - 1), 2)

    for comp in range(COMP):

        def add_res(side, tile):
            scale = 1.25 * diag[tile, face(side), :] * face_w[side, tile]
            value = split[comp, tile, face(side), :] + split[COMP + 1 + comp, tile, face(side), :]
            value = value + scale * halo_vel[NU - 1, side, comp, tile]
            return lambda: keep_parts(comp, tile, face(side), value)

        with_faces(NU, comp, add_res)

    total = add_rows(total, 1, cx - 1, (0, cy - 1), 14)
    total = add_rows(total, 0, 1, range(cy), 1)
    total = add_rows(total, cx - 1, cx, range(cy), 1)

    total = total[: PACKED // 2] + total[PACKED // 2 :]
    for comp in range(COMP + 1):
        for half in range(2):
            start = comp * HIGH + half * TILES
            part[comp * TILES : (comp + 1) * TILES, half * LOW : (half + 1) * LOW] = total[
                start : start + TILES
            ]
    part[SUMS : SUMS + 8, :] = jnp.full((8, LANES), own_ref[0, 0], jnp.int32).astype(jnp.float32)

    def share(step):
        return pltpu.make_async_remote_copy(
            src_ref=part,
            dst_ref=gathered.at[step],
            send_sem=all_send.at[step],
            recv_sem=all_recv.at[step],
            device_id=(lax.rem(gx + step, n_gx), gy),
            device_id_type=MESH,
        )

    for step in range(1, n_gx):
        share(step).start()

    base = lax.div(gx, GROUP) * GROUP
    member = lax.broadcasted_iota(jnp.int32, (GROUP, LANES), 0)
    owner_of = (base + member).astype(jnp.float32)
    tiles = [jnp.zeros((GROUP, LANES), jnp.float32) for _ in range(SUMS)]
    for step in range(n_gx):
        if step:
            share(step).wait_recv()
        source = gathered.at[step] if step else part
        mine = source[SUMS : SUMS + 8, :] == owner_of
        for at in range(SUMS):
            row = jnp.broadcast_to(source[at : at + 1, :], (GROUP, LANES))
            tiles[at] = tiles[at] + jnp.where(mine, row, 0.0)
    for at in range(SUMS):
        owned_ref[at] = tiles[at]
    drain(0)
    for turn in range(1, NU + 1):
        for comp in range(COMP):
            drain(turn, comp)
    for step in range(1, n_gx):
        share(step).wait_send()
    for store in stores:
        store.wait()


def coarse_kernel(vel_in, owned_ref, vel_out, cor_ref, sem):
    copies = [
        pltpu.make_async_copy(vel_in.at[comp], vel_out.at[comp], sem.at[comp])
        for comp in range(COMP)
    ]
    for copy in copies:
        copy.start()
    gx = lax.axis_index("gx")
    base = lax.div(gx, GROUP) * GROUP
    owned = [
        jnp.concatenate([owned_ref[comp * TILES + at] for at in range(TILES)], axis=1)
        for comp in range(COMP + 1)
    ]
    coarse_res, coarse_diag = owned[:COMP], 1.0 + owned[COMP]
    lane = lax.broadcasted_iota(jnp.int32, (GROUP, NAGG), 1)
    member = lax.broadcasted_iota(jnp.int32, (GROUP, NAGG), 0)
    own_row = member == gx - base

    def partner(value, level):
        apart = 2**level
        odd = lax.rem(lax.div(member, apart), 2) == 1
        return jnp.where(
            odd, pltpu.roll(value, apart, 0), pltpu.roll(value, GROUP - apart, 0)
        )

    for level in range(MERGES + 1):
        coupling = 0.2 * jnp.minimum(coarse_diag, pltpu.roll(coarse_diag, NAGG - 1, 1))
        coupling = jnp.where(lane == NAGG - 1, 0.0, coupling)
        below = pltpu.roll(coupling, 1, 1)
        scale = 0.8 / coarse_diag

        def left(resid, vector):
            image = (
                coarse_diag * vector
                - coupling * pltpu.roll(vector, NAGG - 1, 1)
                - below * pltpu.roll(vector, 1, 1)
            )
            return resid - image

        merged = []
        for comp in range(COMP):
            resid = coarse_res[comp]
            error = scale * resid
            error = error + scale * left(resid, error)
            cor_ref[0, 0, comp, level : level + 1, :] = jnp.sum(
                jnp.where(own_row, error, 0.0), axis=0, keepdims=True
            )
            if level < MERGES:
                rest = left(resid, error)
                merged.append(rest + partner(rest, level))
        if level < MERGES:
            coarse_res = merged
            coarse_diag = coarse_diag + partner(coarse_diag, level)

    for copy in copies:
        copy.wait()


def shards(n_gx, n_gy, right_side, viscosity, reaction, agg_ids, owner_map):
    comp, cx, cy, cz = right_side.shape
    rows = cx * cy
    whole = (rows, cz)
    tiles_z = cz // LANES
    inside = (tiles_z, rows, LANES)
    rimmed = (tiles_z, rows + 2 * cy, LANES)
    face = (tiles_z, cx, LANES)
    hbm = pl.BlockSpec(memory_space=pltpu.HBM)
    f32 = jnp.float32

    def stay(array):
        return pltpu.with_memory_space_constraint(array, pltpu.HBM)

    velocity, owned = pl.pallas_call(
        functools.partial(kernel, (n_gx, n_gy, cx, cy, cz)),
        out_shape=(
            jax.ShapeDtypeStruct((comp,) + whole, f32),
            jax.ShapeDtypeStruct((SUMS, GROUP, LANES), f32),
        ),
        in_specs=[hbm] * 4 + [pl.BlockSpec(memory_space=pltpu.SMEM)],
        out_specs=(pl.BlockSpec(memory_space=pl.ANY), pl.BlockSpec(memory_space=pltpu.VMEM)),
        scratch_shapes=[
            pltpu.VMEM((comp,) + inside, f32),
            pltpu.VMEM(rimmed, f32),
            pltpu.VMEM(inside, f32),
            pltpu.VMEM(inside, f32),
            pltpu.VMEM(inside, jnp.int32),
            pltpu.VMEM(inside, f32),
            pltpu.VMEM(inside, f32),
            pltpu.VMEM((6,) + inside, f32),
            [pltpu.VMEM((comp,) + rimmed, f32)] * NU,
            pltpu.VMEM((2 * (comp + 1),) + inside, f32),
            pltpu.VMEM((4,) + face, f32),
            pltpu.VMEM((2,) + face, f32),
            pltpu.VMEM((NU, 4, comp) + face, f32),
            pltpu.VMEM((NU, 2, comp) + face, f32),
            pltpu.VMEM((4,) + face, f32),
            pltpu.VMEM((SUMS + 8, LANES), f32),
            pltpu.VMEM((n_gx, SUMS + 8, LANES), f32),
            pltpu.SemaphoreType.DMA((4, tiles_z)),
            pltpu.SemaphoreType.DMA((tiles_z,)),
            pltpu.SemaphoreType.DMA((NU + 1, 4, COMP)),
            pltpu.SemaphoreType.DMA((NU + 1, 4, COMP)),
            pltpu.SemaphoreType.DMA((n_gx,)),
            pltpu.SemaphoreType.DMA((n_gx,)),
        ],
        compiler_params=pltpu.CompilerParams(
            collective_id=0, has_side_effects=True, vmem_limit_bytes=30 * 2**20
        ),
    )(
        stay(right_side.reshape((comp,) + whole)),
        stay(viscosity.reshape(whole)),
        stay(reaction.reshape(whole)),
        stay(agg_ids.reshape(whole)),
        owner_map,
    )
    velocity, levels = pl.pallas_call(
        coarse_kernel,
        out_shape=(
            jax.ShapeDtypeStruct((comp,) + whole, f32),
            jax.ShapeDtypeStruct((1, 1, comp, MERGES + 1, NAGG), f32),
        ),
        in_specs=[pl.BlockSpec(memory_space=pl.ANY), pl.BlockSpec(memory_space=pltpu.VMEM)],
        out_specs=(hbm, pl.BlockSpec(memory_space=pltpu.VMEM)),
        scratch_shapes=[pltpu.SemaphoreType.DMA((COMP,))],
        compiler_params=pltpu.CompilerParams(vmem_limit_bytes=8 * 2**20),
    )(velocity, owned)
    return velocity.reshape(right_side.shape), levels.transpose(0, 1, 3, 2, 4)


def solution(mesh):
    return jax.shard_map(
        functools.partial(shards, mesh.shape["gx"], mesh.shape["gy"]),
        mesh=mesh,
        in_specs=(
            P(None, "gx", "gy", None),
            P("gx", "gy", None),
            P("gx", "gy", None),
            P("gx", "gy", None),
            P("gx", "gy"),
        ),
        out_specs=(P(None, "gx", "gy", None), P("gx", "gy", None, None, None)),
        check_vma=False,
    )
```

```python
import functools

import jax
import jax.numpy as jnp
from jax import lax
from jax.experimental import pallas as pl
from jax.experimental.pallas import tpu as pltpu
from jax.sharding import PartitionSpec as P

COMP = 3
NAGG = 512
NU = 3
MERGES = 3
GROUP = 2**MERGES
LANES = 128
LOW = 64
HIGH = NAGG // LOW
PACKED = 2 * (COMP + 1) * HIGH
TILES = NAGG // LANES
SUMS = (COMP + 1) * TILES
MESH = pl.DeviceIdType.MESH


def kernel(
    dims,
    rs_hbm,
    visc_hbm,
    reac_hbm,
    ids_hbm,
    own_ref,
    vel_hbm,
    owned_ref,
    rs,
    visc,
    reac,
    diag,
    ids,
    low_ids,
    high_ids,
    weight,
    vel,
    split,
    halo_visc,
    pack_visc,
    halo_vel,
    pack_vel,
    face_w,
    part,
    gathered,
    load_sem,
    store_sem,
    send_sem,
    recv_sem,
    all_send,
    all_recv,
):
    n_gx, n_gy, cx, cy, cz = dims
    rows = cx * cy
    tiles_z = cz // LANES
    gx, gy = lax.axis_index("gx"), lax.axis_index("gy")
    has = (gx > 0, gx < n_gx - 1, gy > 0, gy < n_gy - 1)
    targets = ((gx - 1, gy), (gx + 1, gy), (gx, gy - 1), (gx, gy + 1))

    def face(side, before=0):
        if side < 2:
            return pl.ds(before + (rows - cy if side else 0), cy)
        return pl.ds(before + (cy - 1 if side == 3 else 0), cx, stride=cy)

    block = pl.ds(cy, rows)
    sources = (visc_hbm, reac_hbm, ids_hbm, rs_hbm)
    loads = []
    for which, src in enumerate(sources):
        pieces = []
        for tile in range(tiles_z):
            lanes = pl.ds(tile * LANES, LANES)
            if which == 0:
                ends = src.at[:, lanes], visc.at[tile, block, :]
            elif which == 3:
                ends = src.at[:, :, lanes], rs.at[:, tile]
            else:
                ends = src.at[:, lanes], (reac if which == 1 else ids).at[tile]
            pieces.append(pltpu.make_async_copy(*ends, load_sem.at[which, tile]))
        loads.append(pieces)
    for pieces in loads:
        for piece in pieces:
            piece.start()

    def arrived(which):
        for piece in loads[which]:
            piece.wait()

    barrier = pltpu.get_barrier_semaphore()
    for step in range(1, n_gx):
        pl.semaphore_signal(
            barrier, inc=1, device_id=(lax.rem(gx + step, n_gx), gy), device_id_type=MESH
        )
    for side in (2, 3):

        @pl.when(has[side])
        def _():
            pl.semaphore_signal(barrier, inc=1, device_id=targets[side], device_id_type=MESH)

    empty = jnp.zeros((cy, LANES), jnp.float32)
    for tile in range(tiles_z):
        for rim in (0, rows + cy):
            visc[tile, rim : rim + cy, :] = empty
            for turn in range(NU):
                for comp in range(COMP):
                    vel[turn][comp, tile, rim : rim + cy, :] = empty

    arrived(0)
    for side in (2, 3):
        for tile in range(tiles_z):
            pack_visc[side - 2, tile] = visc[tile, face(side, cy), :]
    waits = (n_gx - 1) + has[2].astype(jnp.int32) + has[3].astype(jnp.int32)
    pl.semaphore_wait(barrier, waits)

    def face_copy(turn, side, comp=0):
        other = side ^ 1
        if turn == 0:
            src = visc.at[:, face(side, cy), :] if side < 2 else pack_visc.at[side - 2]
            dst = halo_visc.at[other]
        else:
            src = (
                vel[turn - 1].at[comp, :, face(side, cy), :]
                if side < 2
                else pack_vel.at[turn - 1, side - 2, comp]
            )
            dst = halo_vel.at[turn - 1, other, comp]
        return pltpu.make_async_remote_copy(
            src_ref=src,
            dst_ref=dst,
            send_sem=send_sem.at[turn, side, comp],
            recv_sem=recv_sem.at[turn, other, comp],
            device_id=targets[side],
            device_id_type=MESH,
        )

    def send_faces(turn, comp=0, sides=(2, 3, 0, 1), pack=True):
        for side in sides:

            @pl.when(has[side])
            def _():
                if turn and side >= 2 and pack:
                    for tile in range(tiles_z):
                        pack_vel[turn - 1, side - 2, comp, tile] = vel[turn - 1][comp, tile, face(side, cy), :
                        ]
                face_copy(turn, side, comp).start()

    def with_faces(turn, comp, work):
        for side in range(4):

            @pl.when(has[side])
            def _():
                face_copy(turn, side ^ 1, comp).wait_recv()
                stores = [work(side, tile) for tile in range(tiles_z)]
                for store in stores:
                    store()

    def drain(turn, comp=0):
        for side in range(4):

            @pl.when(has[side])
            def _():
                face_copy(turn, side, comp).wait_send()

    send_faces(0)
    shape = (cy, LANES)
    row_at = lax.broadcasted_iota(jnp.int32, shape, 0)
    lane_at = lax.broadcasted_iota(jnp.int32, shape, 1)
    no_high_y, no_low_y = row_at == cy - 1, row_at == 0
    last_lane, first_lane = lane_at == LANES - 1, lane_at == 0

    def plane(at, before=0):
        start = at * cy if isinstance(at, int) else pl.multiple_of(at * cy, cy)
        return pl.ds(start + before, cy)

    def beside_z(pieces, tile):
        here = pieces[tile]
        above = jnp.where(first_lane, pieces[(tile + 1) % tiles_z], here)
        under = jnp.where(last_lane, pieces[tile - 1], here)
        return pltpu.roll(above, LANES - 1, 1), pltpu.roll(under, 1, 1)

    def visc_beside(at, tile, pieces):
        high_z, low_z = beside_z(pieces, tile)
        if tile == tiles_z - 1:
            high_z = jnp.where(last_lane, 0.0, high_z)
        if tile == 0:
            low_z = jnp.where(first_lane, 0.0, low_z)
        return (
            visc[tile, plane(at, 2 * cy), :],
            visc[tile, plane(at), :],
            jnp.where(no_high_y, 0.0, visc[tile, plane(at, cy + 1), :]),
            jnp.where(no_low_y, 0.0, visc[tile, plane(at, cy - 1), :]),
            high_z,
            low_z,
        )

    def planes(start, end, together):
        def each(work):
            together_now = together
            while (end - start) % together_now:
                together_now -= 1

            @pl.loop(0, (end - start) // together_now)
            def _(turn):
                for inner in range(together_now):
                    work(start + turn * together_now + inner)

        return each

    arrived(1)
    arrived(2)

    @planes(0, cx, 4)
    def _(at):
        for tile in range(tiles_z):
            label = ids[tile, plane(at), :]
            low_ids[tile, plane(at), :] = (label & (LOW - 1)).astype(jnp.float32)
            high = lax.shift_right_logical(label, LOW.bit_length() - 1)
            high_ids[tile, plane(at), :] = high.astype(jnp.float32)
        pieces = [visc[tile, plane(at, cy), :] for tile in range(tiles_z)]
        for tile in range(tiles_z):
            total = functools.reduce(jnp.add, visc_beside(at, tile, pieces))
            diag[tile, plane(at), :] = (
                reac[tile, plane(at), :] + 3.0 * pieces[tile] + 0.5 * total
            )

    def keep_parts(comp, tile, where, value):
        upper = value.astype(jnp.bfloat16).astype(jnp.float32)
        split[comp, tile, where, :] = upper
        split[COMP + 1 + comp, tile, where, :] = value - upper

    def add_visc(side, tile):
        value = diag[tile, face(side), :] + 0.5 * halo_visc[side, tile]

        def store():
            diag[tile, face(side), :] = value

        return store

    with_faces(0, 0, add_visc)
    arrived(3)

    for side in (2, 3):

        @pl.when(has[side])
        def _():
            for tile in range(tiles_z):
                scale = 0.8 / diag[tile, face(side), :]
                for comp in range(COMP):
                    pack_vel[0, side - 2, comp, tile] = scale * rs[comp, tile, face(side), :]

    for comp in range(COMP):
        send_faces(1, comp, (2, 3), False)

    def scale_plane(at):
        pieces = [visc[tile, plane(at, cy), :] for tile in range(tiles_z)]
        for tile in range(tiles_z):
            here = pieces[tile]
            scale = 0.8 / diag[tile, plane(at), :]
            keep_parts(COMP, tile, plane(at), diag[tile, plane(at), :])
            for comp in range(COMP):
                vel[0][comp, tile, plane(at, cy), :] = scale * rs[comp, tile, plane(at), :]
            half = 0.5 * scale
            found = visc_beside(at, tile, pieces)
            drops = [None, None, no_high_y, no_low_y, None, None]
            if tile == tiles_z - 1:
                drops[4] = last_lane
            if tile == 0:
                drops[5] = first_lane
            for which, (other, drop) in enumerate(zip(found, drops)):
                ratio = half * (here + other)
                if drop is not None:
                    ratio = jnp.where(drop, 0.0, ratio)
                weight[which, tile, plane(at), :] = ratio

    scale_plane(0)
    scale_plane(cx - 1)
    for comp in range(COMP):
        send_faces(1, comp, (0, 1))
    planes(1, cx - 1, 7)(scale_plane)
    for side in range(4):

        @pl.when(has[side])
        def _():
            for tile in range(tiles_z):
                face_w[side, tile] = (
                    0.4
                    / diag[tile, face(side), :]
                    * (visc[tile, face(side, cy), :] + halo_visc[side, tile])
                )

    def from_beside(turn, at, write, comps):
        pieces = {
            comp: [vel[turn][comp, tile, plane(at, cy), :] for tile in range(tiles_z)]
            for comp in comps
        }
        for tile in range(tiles_z):
            ratios = [weight[which, tile, plane(at), :] for which in range(6)]
            for comp in comps:
                high_z, low_z = beside_z(pieces[comp], tile)
                total = ratios[0] * vel[turn][comp, tile, plane(at, 2 * cy), :]
                total += ratios[1] * vel[turn][comp, tile, plane(at), :]
                total += ratios[2] * vel[turn][comp, tile, plane(at, cy + 1), :]
                total += ratios[3] * vel[turn][comp, tile, plane(at, cy - 1), :]
                total += ratios[4] * high_z + ratios[5] * low_z
                write(comp, tile, pieces[comp][tile], total)

    def sweep(turn, comp):
        @planes(0, cx, 8)
        def _(at):
            def write(comp, tile, here, total):
                first = vel[0][comp, tile, plane(at, cy), :]
                vel[turn][comp, tile, plane(at, cy), :] = first + 0.2 * here + total

            from_beside(turn - 1, at, write, (comp,))

        def add_vel(side, tile):
            value = (
                vel[turn][comp, tile, face(side, cy), :]
                + face_w[side, tile] * halo_vel[turn - 1, side, comp, tile]
            )

            def store():
                vel[turn][comp, tile, face(side, cy), :] = value

            return store

        with_faces(turn, comp, add_vel)
        send_faces(turn + 1, comp)

    for turn in range(1, NU):
        for comp in range(COMP):
            sweep(turn, comp)

    stores = [
        pltpu.make_async_copy(
            vel[NU - 1].at[:, tile, block, :],
            vel_hbm.at[:, :, pl.ds(tile * LANES, LANES)],
            store_sem.at[tile],
        )
        for tile in range(tiles_z)
    ]
    for store in stores:
        store.start()

    @planes(0, cx, 4)
    def _(at):
        def write(comp, tile, here, total):
            scale = 1.25 * diag[tile, plane(at), :]
            first = vel[0][comp, tile, plane(at, cy), :]
            keep_parts(comp, tile, plane(at), scale * (first - 0.8 * here + total))

        from_beside(NU - 1, at, write, range(COMP))

    high_at = lax.broadcasted_iota(jnp.int32, (16, LANES), 0) & (HIGH - 1)
    high_at = 2 * (high_at & (TILES - 1)) + lax.shift_right_logical(high_at, 2)
    high_at = high_at.astype(jnp.float32).astype(jnp.bfloat16)
    low_at = lax.broadcasted_iota(jnp.int32, (LOW, LANES), 0).astype(jnp.float32)
    low_at = low_at.astype(jnp.bfloat16)
    one, zero = jnp.ones((), jnp.bfloat16), jnp.zeros((), jnp.bfloat16)

    def add_pair(total, pair_rows):
        tables, parts = [], []
        for row, tile in [(row, tile) for row in pair_rows for tile in range(tiles_z)]:

            def spread(first, second):
                both = [jnp.broadcast_to(each, (HIGH, LANES)) for each in (first, second)]
                return jnp.concatenate(both, axis=0).astype(jnp.bfloat16)

            low = low_ids[tile, pl.ds(row, 1), :]
            low = jnp.concatenate([spread(low, low)] * (LOW // 16), axis=0)
            tables.append(jnp.where(low == low_at, one, zero))
            high = high_ids[tile, pl.ds(row, 1), :]
            is_high = spread(high, high) == high_at
            kept = []
            for at in range(0, 2 * (COMP + 1), 2):
                pair = spread(
                    split[at, tile, pl.ds(row, 1), :], split[at + 1, tile, pl.ds(row, 1), :]
                )
                kept.append(jnp.where(is_high, pair, zero))
            parts.append(jnp.concatenate(kept, axis=0))
        return total + lax.dot_general(
            jnp.concatenate(parts, axis=1),
            jnp.concatenate(tables, axis=1),
            (((1,), (1,)), ((), ())),
            preferred_element_type=jnp.float32,
        )

    def add_rows(total, start, end, within, together):
        while (end - start) % together:
            together -= 1

        def body(turn, carried):
            todo = [
                (start + turn * together + inner) * cy + row
                for inner in range(together)
                for row in within
            ]
            for first in range(0, len(todo), 2):
                carried = add_pair(carried, todo[first : first + 2])
            return carried

        count = (end - start) // together
        return body(0, total) if count == 1 else lax.fori_loop(0, count, body, total)

    total = jnp.zeros((PACKED, LOW), jnp.float32)
    total = add_rows(total, 1, cx - 1, range(1, cy - 1), 2)

    for comp in range(COMP):

        def add_res(side, tile):
            scale = 1.25 * diag[tile, face(side), :] * face_w[side, tile]
            value = split[comp, tile, face(side), :] + split[COMP + 1 + comp, tile, face(side), :]
            value = value + scale * halo_vel[NU - 1, side, comp, tile]
            return lambda: keep_parts(comp, tile, face(side), value)

        with_faces(NU, comp, add_res)

    total = add_rows(total, 1, cx - 1, (0, cy - 1), 14)
    total = add_rows(total, 0, 1, range(cy), 1)
    total = add_rows(total, cx - 1, cx, range(cy), 1)

    total = total[: PACKED // 2] + total[PACKED // 2 :]
    for comp in range(COMP + 1):
        for half in range(2):
            start = comp * HIGH + half * TILES
            part[comp * TILES : (comp + 1) * TILES, half * LOW : (half + 1) * LOW] = total[
                start : start + TILES
            ]
    part[SUMS : SUMS + 8, :] = jnp.full((8, LANES), own_ref[0, 0], jnp.int32).astype(jnp.float32)

    def share(step):
        return pltpu.make_async_remote_copy(
            src_ref=part,
            dst_ref=gathered.at[step],
            send_sem=all_send.at[step],
            recv_sem=all_recv.at[step],
            device_id=(lax.rem(gx + step, n_gx), gy),
            device_id_type=MESH,
        )

    for step in range(1, n_gx):
        share(step).start()

    base = lax.div(gx, GROUP) * GROUP
    member = lax.broadcasted_iota(jnp.int32, (GROUP, LANES), 0)
    owner_of = (base + member).astype(jnp.float32)
    tiles = [jnp.zeros((GROUP, LANES), jnp.float32) for _ in range(SUMS)]
    for step in range(n_gx):
        if step:
            share(step).wait_recv()
        source = gathered.at[step] if step else part
        mine = source[SUMS : SUMS + 8, :] == owner_of
        for at in range(SUMS):
            row = jnp.broadcast_to(source[at : at + 1, :], (GROUP, LANES))
            tiles[at] = tiles[at] + jnp.where(mine, row, 0.0)
    for at in range(SUMS):
        owned_ref[at] = tiles[at]
    drain(0)
    for turn in range(1, NU + 1):
        for comp in range(COMP):
            drain(turn, comp)
    for step in range(1, n_gx):
        share(step).wait_send()
    for store in stores:
        store.wait()


def coarse_kernel(vel_in, owned_ref, vel_out, cor_ref, sem):
    copies = [
        pltpu.make_async_copy(vel_in.at[comp], vel_out.at[comp], sem.at[comp])
        for comp in range(COMP)
    ]
    for copy in copies:
        copy.start()
    gx = lax.axis_index("gx")
    base = lax.div(gx, GROUP) * GROUP
    owned = [
        jnp.concatenate([owned_ref[comp * TILES + at] for at in range(TILES)], axis=1)
        for comp in range(COMP + 1)
    ]
    coarse_res, coarse_diag = owned[:COMP], 1.0 + owned[COMP]
    lane = lax.broadcasted_iota(jnp.int32, (GROUP, NAGG), 1)
    member = lax.broadcasted_iota(jnp.int32, (GROUP, NAGG), 0)
    own_row = member == gx - base

    def partner(value, level):
        apart = 2**level
        odd = lax.rem(lax.div(member, apart), 2) == 1
        return jnp.where(
            odd, pltpu.roll(value, apart, 0), pltpu.roll(value, GROUP - apart, 0)
        )

    for level in range(MERGES + 1):
        coupling = 0.2 * jnp.minimum(coarse_diag, pltpu.roll(coarse_diag, NAGG - 1, 1))
        coupling = jnp.where(lane == NAGG - 1, 0.0, coupling)
        below = pltpu.roll(coupling, 1, 1)
        scale = 0.8 / coarse_diag

        def left(resid, vector):
            image = (
                coarse_diag * vector
                - coupling * pltpu.roll(vector, NAGG - 1, 1)
                - below * pltpu.roll(vector, 1, 1)
            )
            return resid - image

        merged = []
        for comp in range(COMP):
            resid = coarse_res[comp]
            error = scale * resid
            error = error + scale * left(resid, error)
            cor_ref[0, 0, comp, level : level + 1, :] = jnp.sum(
                jnp.where(own_row, error, 0.0), axis=0, keepdims=True
            )
            if level < MERGES:
                rest = left(resid, error)
                merged.append(rest + partner(rest, level))
        if level < MERGES:
            coarse_res = merged
            coarse_diag = coarse_diag + partner(coarse_diag, level)

    for copy in copies:
        copy.wait()


def shards(n_gx, n_gy, right_side, viscosity, reaction, agg_ids, owner_map):
    comp, cx, cy, cz = right_side.shape
    rows = cx * cy
    whole = (rows, cz)
    tiles_z = cz // LANES
    inside = (tiles_z, rows, LANES)
    rimmed = (tiles_z, rows + 2 * cy, LANES)
    face = (tiles_z, cx, LANES)
    hbm = pl.BlockSpec(memory_space=pltpu.HBM)
    f32 = jnp.float32

    def stay(array):
        return pltpu.with_memory_space_constraint(array, pltpu.HBM)

    velocity, owned = pl.pallas_call(
        functools.partial(kernel, (n_gx, n_gy, cx, cy, cz)),
        out_shape=(
            jax.ShapeDtypeStruct((comp,) + whole, f32),
            jax.ShapeDtypeStruct((SUMS, GROUP, LANES), f32),
        ),
        in_specs=[hbm] * 4 + [pl.BlockSpec(memory_space=pltpu.SMEM)],
        out_specs=(pl.BlockSpec(memory_space=pl.ANY), pl.BlockSpec(memory_space=pltpu.VMEM)),
        scratch_shapes=[
            pltpu.VMEM((comp,) + inside, f32),
            pltpu.VMEM(rimmed, f32),
            pltpu.VMEM(inside, f32),
            pltpu.VMEM(inside, f32),
            pltpu.VMEM(inside, jnp.int32),
            pltpu.VMEM(inside, f32),
            pltpu.VMEM(inside, f32),
            pltpu.VMEM((6,) + inside, f32),
            [pltpu.VMEM((comp,) + rimmed, f32)] * NU,
            pltpu.VMEM((2 * (comp + 1),) + inside, f32),
            pltpu.VMEM((4,) + face, f32),
            pltpu.VMEM((2,) + face, f32),
            pltpu.VMEM((NU, 4, comp) + face, f32),
            pltpu.VMEM((NU, 2, comp) + face, f32),
            pltpu.VMEM((4,) + face, f32),
            pltpu.VMEM((SUMS + 8, LANES), f32),
            pltpu.VMEM((n_gx, SUMS + 8, LANES), f32),
            pltpu.SemaphoreType.DMA((4, tiles_z)),
            pltpu.SemaphoreType.DMA((tiles_z,)),
            pltpu.SemaphoreType.DMA((NU + 1, 4, COMP)),
            pltpu.SemaphoreType.DMA((NU + 1, 4, COMP)),
            pltpu.SemaphoreType.DMA((n_gx,)),
            pltpu.SemaphoreType.DMA((n_gx,)),
        ],
        compiler_params=pltpu.CompilerParams(
            collective_id=0, has_side_effects=True, vmem_limit_bytes=30 * 2**20
        ),
    )(
        stay(right_side.reshape((comp,) + whole)),
        stay(viscosity.reshape(whole)),
        stay(reaction.reshape(whole)),
        stay(agg_ids.reshape(whole)),
        owner_map,
    )
    velocity, levels = pl.pallas_call(
        coarse_kernel,
        out_shape=(
            jax.ShapeDtypeStruct((comp,) + whole, f32),
            jax.ShapeDtypeStruct((1, 1, comp, MERGES + 1, NAGG), f32),
        ),
        in_specs=[pl.BlockSpec(memory_space=pl.ANY), pl.BlockSpec(memory_space=pltpu.VMEM)],
        out_specs=(hbm, pl.BlockSpec(memory_space=pltpu.VMEM)),
        scratch_shapes=[pltpu.SemaphoreType.DMA((COMP,))],
        compiler_params=pltpu.CompilerParams(vmem_limit_bytes=8 * 2**20),
    )(velocity, owned)
    return velocity.reshape(right_side.shape), levels.transpose(0, 1, 3, 2, 4)


def solution(mesh):
    return jax.shard_map(
        functools.partial(shards, mesh.shape["gx"], mesh.shape["gy"]),
        mesh=mesh,
        in_specs=(
            P(None, "gx", "gy", None),
            P("gx", "gy", None),
            P("gx", "gy", None),
            P("gx", "gy", None),
            P("gx", "gy"),
        ),
        out_specs=(P(None, "gx", "gy", None), P("gx", "gy", None, None, None)),
        check_vma=False,
    )
```

```python
import functools

import jax
import jax.numpy as jnp
from jax import lax
from jax.experimental import pallas as pl
from jax.experimental.pallas import tpu as pltpu
from jax.sharding import PartitionSpec as P

COMP = 3
NAGG = 512
NU = 3
MERGES = 3
GROUP = 2**MERGES
CHAINS = 2
LANES = 128
LOW = 64
HIGH = NAGG // LOW
PACKED = 2 * (COMP + 1) * HIGH
TILES = NAGG // LANES
SUMS = (COMP + 1) * TILES
MESH = pl.DeviceIdType.MESH


def kernel(
    dims,
    rs_hbm,
    visc_hbm,
    reac_hbm,
    ids_hbm,
    own_ref,
    vel_hbm,
    owned_ref,
    rs,
    visc,
    reac,
    diag,
    ids,
    low_ids,
    high_ids,
    weight,
    vel,
    split,
    halo_visc,
    pack_visc,
    halo_vel,
    pack_vel,
    face_w,
    part,
    gathered,
    load_sem,
    store_sem,
    send_sem,
    recv_sem,
    all_send,
    all_recv,
):
    n_gx, n_gy, cx, cy, cz = dims
    rows = cx * cy
    tiles_z = cz // LANES
    gx, gy = lax.axis_index("gx"), lax.axis_index("gy")
    has = (gx > 0, gx < n_gx - 1, gy > 0, gy < n_gy - 1)
    targets = ((gx - 1, gy), (gx + 1, gy), (gx, gy - 1), (gx, gy + 1))

    def face(side, before=0):
        if side < 2:
            return pl.ds(before + (rows - cy if side else 0), cy)
        return pl.ds(before + (cy - 1 if side == 3 else 0), cx, stride=cy)

    block = pl.ds(cy, rows)
    sources = (visc_hbm, reac_hbm, ids_hbm, rs_hbm)
    loads = []
    for which, src in enumerate(sources):
        pieces = []
        for tile in range(tiles_z):
            lanes = pl.ds(tile * LANES, LANES)
            if which == 0:
                ends = src.at[:, lanes], visc.at[tile, block, :]
            elif which == 3:
                ends = src.at[:, :, lanes], rs.at[:, tile]
            else:
                ends = src.at[:, lanes], (reac if which == 1 else ids).at[tile]
            pieces.append(pltpu.make_async_copy(*ends, load_sem.at[which, tile]))
        loads.append(pieces)
    for piece in loads[0]:
        piece.start()

    def arrived(which):
        for piece in loads[which]:
            piece.wait()

    barrier = pltpu.get_barrier_semaphore()
    for step in range(1, n_gx):
        pl.semaphore_signal(
            barrier, inc=1, device_id=(lax.rem(gx + step, n_gx), gy), device_id_type=MESH
        )
    for side in (2, 3):

        @pl.when(has[side])
        def _():
            pl.semaphore_signal(barrier, inc=1, device_id=targets[side], device_id_type=MESH)

    for pieces in loads[1:]:
        for piece in pieces:
            piece.start()

    empty = jnp.zeros((cy, LANES), jnp.float32)
    for tile in range(tiles_z):
        for rim in (0, rows + cy):
            visc[tile, rim : rim + cy, :] = empty
            for turn in range(NU):
                for comp in range(COMP):
                    vel[turn][comp, tile, rim : rim + cy, :] = empty

    arrived(0)
    for side in (2, 3):
        for tile in range(tiles_z):
            pack_visc[side - 2, tile] = visc[tile, face(side, cy), :]
    waits = (n_gx - 1) + has[2].astype(jnp.int32) + has[3].astype(jnp.int32)
    pl.semaphore_wait(barrier, waits)

    def face_copy(turn, side, comp=0):
        other = side ^ 1
        if turn == 0:
            src = visc.at[:, face(side, cy), :] if side < 2 else pack_visc.at[side - 2]
            dst = halo_visc.at[other]
        else:
            src = (
                vel[turn - 1].at[comp, :, face(side, cy), :]
                if side < 2
                else pack_vel.at[turn - 1, side - 2, comp]
            )
            dst = halo_vel.at[turn - 1, other, comp]
        return pltpu.make_async_remote_copy(
            src_ref=src,
            dst_ref=dst,
            send_sem=send_sem.at[turn, side, comp],
            recv_sem=recv_sem.at[turn, other, comp],
            device_id=targets[side],
            device_id_type=MESH,
        )

    def send_faces(turn, comp=0, sides=(2, 3, 0, 1), pack=True):
        for side in sides:

            @pl.when(has[side])
            def _():
                if turn and side >= 2 and pack:
                    for tile in range(tiles_z):
                        pack_vel[turn - 1, side - 2, comp, tile] = vel[turn - 1][comp, tile, face(side, cy), :
                        ]
                face_copy(turn, side, comp).start()

    def with_faces(turn, comp, work):
        for side in range(4):

            @pl.when(has[side])
            def _():
                face_copy(turn, side ^ 1, comp).wait_recv()
                stores = [work(side, tile) for tile in range(tiles_z)]
                for store in stores:
                    store()

    def drain(turn, comp=0):
        for side in range(4):

            @pl.when(has[side])
            def _():
                face_copy(turn, side, comp).wait_send()

    send_faces(0)
    shape = (cy, LANES)
    row_at = lax.broadcasted_iota(jnp.int32, shape, 0)
    lane_at = lax.broadcasted_iota(jnp.int32, shape, 1)
    no_high_y, no_low_y = row_at == cy - 1, row_at == 0
    last_lane, first_lane = lane_at == LANES - 1, lane_at == 0

    def plane(at, before=0):
        start = at * cy if isinstance(at, int) else pl.multiple_of(at * cy, cy)
        return pl.ds(start + before, cy)

    def beside_z(pieces, tile):
        here = pieces[tile]
        above = jnp.where(first_lane, pieces[(tile + 1) % tiles_z], here)
        under = jnp.where(last_lane, pieces[tile - 1], here)
        return pltpu.roll(above, LANES - 1, 1), pltpu.roll(under, 1, 1)

    def visc_beside(at, tile, pieces):
        high_z, low_z = beside_z(pieces, tile)
        if tile == tiles_z - 1:
            high_z = jnp.where(last_lane, 0.0, high_z)
        if tile == 0:
            low_z = jnp.where(first_lane, 0.0, low_z)
        return (
            visc[tile, plane(at, 2 * cy), :],
            visc[tile, plane(at), :],
            jnp.where(no_high_y, 0.0, visc[tile, plane(at, cy + 1), :]),
            jnp.where(no_low_y, 0.0, visc[tile, plane(at, cy - 1), :]),
            high_z,
            low_z,
        )

    def planes(start, end, together):
        def each(work):
            together_now = together
            while (end - start) % together_now:
                together_now -= 1

            @pl.loop(0, (end - start) // together_now)
            def _(turn):
                for inner in range(together_now):
                    work(start + turn * together_now + inner)

        return each

    arrived(1)
    arrived(2)

    @planes(0, cx, 4)
    def _(at):
        for tile in range(tiles_z):
            label = ids[tile, plane(at), :]
            low_ids[tile, plane(at), :] = (label & (LOW - 1)).astype(jnp.float32)
            high = lax.shift_right_logical(label, LOW.bit_length() - 1)
            high_ids[tile, plane(at), :] = high.astype(jnp.float32)
        pieces = [visc[tile, plane(at, cy), :] for tile in range(tiles_z)]
        for tile in range(tiles_z):
            total = functools.reduce(jnp.add, visc_beside(at, tile, pieces))
            diag[tile, plane(at), :] = (
                reac[tile, plane(at), :] + 3.0 * pieces[tile] + 0.5 * total
            )

    def keep_parts(comp, tile, where, value):
        upper = value.astype(jnp.bfloat16).astype(jnp.float32)
        split[comp, tile, where, :] = upper
        split[COMP + 1 + comp, tile, where, :] = value - upper

    def add_visc(side, tile):
        value = diag[tile, face(side), :] + 0.5 * halo_visc[side, tile]

        def store():
            diag[tile, face(side), :] = value

        return store

    with_faces(0, 0, add_visc)
    arrived(3)

    for side in (2, 3):

        @pl.when(has[side])
        def _():
            for tile in range(tiles_z):
                scale = 0.8 / diag[tile, face(side), :]
                for comp in range(COMP):
                    pack_vel[0, side - 2, comp, tile] = scale * rs[comp, tile, face(side), :]

    for comp in range(COMP):
        send_faces(1, comp, (2, 3), False)

    def scale_plane(at):
        pieces = [visc[tile, plane(at, cy), :] for tile in range(tiles_z)]
        for tile in range(tiles_z):
            here = pieces[tile]
            scale = 0.8 / diag[tile, plane(at), :]
            keep_parts(COMP, tile, plane(at), diag[tile, plane(at), :])
            for comp in range(COMP):
                vel[0][comp, tile, plane(at, cy), :] = scale * rs[comp, tile, plane(at), :]
            half = 0.5 * scale
            found = visc_beside(at, tile, pieces)
            drops = [None, None, no_high_y, no_low_y, None, None]
            if tile == tiles_z - 1:
                drops[4] = last_lane
            if tile == 0:
                drops[5] = first_lane
            for which, (other, drop) in enumerate(zip(found, drops)):
                ratio = half * (here + other)
                if drop is not None:
                    ratio = jnp.where(drop, 0.0, ratio)
                weight[which, tile, plane(at), :] = ratio

    scale_plane(0)
    scale_plane(cx - 1)
    for comp in range(COMP):
        send_faces(1, comp, (0, 1))
    planes(1, cx - 1, 7)(scale_plane)
    for side in range(4):

        @pl.when(has[side])
        def _():
            for tile in range(tiles_z):
                face_w[side, tile] = (
                    0.4
                    / diag[tile, face(side), :]
                    * (visc[tile, face(side, cy), :] + halo_visc[side, tile])
                )

    def from_beside(turn, at, write, comps):
        pieces = {
            comp: [vel[turn][comp, tile, plane(at, cy), :] for tile in range(tiles_z)]
            for comp in comps
        }
        for tile in range(tiles_z):
            ratios = [weight[which, tile, plane(at), :] for which in range(6)]
            for comp in comps:
                high_z, low_z = beside_z(pieces[comp], tile)
                total = ratios[0] * vel[turn][comp, tile, plane(at, 2 * cy), :]
                total += ratios[1] * vel[turn][comp, tile, plane(at), :]
                total += ratios[2] * vel[turn][comp, tile, plane(at, cy + 1), :]
                total += ratios[3] * vel[turn][comp, tile, plane(at, cy - 1), :]
                total += ratios[4] * high_z + ratios[5] * low_z
                write(comp, tile, pieces[comp][tile], total)

    def sweep(turn, comp):
        @planes(0, cx, 8)
        def _(at):
            def write(comp, tile, here, total):
                first = vel[0][comp, tile, plane(at, cy), :]
                vel[turn][comp, tile, plane(at, cy), :] = first + 0.2 * here + total

            from_beside(turn - 1, at, write, (comp,))

        def add_vel(side, tile):
            value = (
                vel[turn][comp, tile, face(side, cy), :]
                + face_w[side, tile] * halo_vel[turn - 1, side, comp, tile]
            )

            def store():
                vel[turn][comp, tile, face(side, cy), :] = value

            return store

        with_faces(turn, comp, add_vel)
        send_faces(turn + 1, comp)

    for turn in range(1, NU):
        for comp in range(COMP):
            sweep(turn, comp)

    stores = [
        pltpu.make_async_copy(
            vel[NU - 1].at[:, tile, block, :],
            vel_hbm.at[:, :, pl.ds(tile * LANES, LANES)],
            store_sem.at[tile],
        )
        for tile in range(tiles_z)
    ]
    for store in stores:
        store.start()

    @planes(0, cx, 4)
    def _(at):
        def write(comp, tile, here, total):
            scale = 1.25 * diag[tile, plane(at), :]
            first = vel[0][comp, tile, plane(at, cy), :]
            keep_parts(comp, tile, plane(at), scale * (first - 0.8 * here + total))

        from_beside(NU - 1, at, write, range(COMP))

    high_at = lax.broadcasted_iota(jnp.int32, (16, LANES), 0) & (HIGH - 1)
    high_at = 2 * (high_at & (TILES - 1)) + lax.shift_right_logical(high_at, 2)
    high_at = high_at.astype(jnp.float32).astype(jnp.bfloat16)
    low_at = lax.broadcasted_iota(jnp.int32, (LOW, LANES), 0).astype(jnp.float32)
    low_at = low_at.astype(jnp.bfloat16)
    one, zero = jnp.ones((), jnp.bfloat16), jnp.zeros((), jnp.bfloat16)

    def add_pair(total, pair_rows):
        tables, parts = [], []
        for row, tile in [(row, tile) for row in pair_rows for tile in range(tiles_z)]:

            def spread(first, second):
                both = [jnp.broadcast_to(each, (HIGH, LANES)) for each in (first, second)]
                return jnp.concatenate(both, axis=0).astype(jnp.bfloat16)

            low = low_ids[tile, pl.ds(row, 1), :]
            low = jnp.concatenate([spread(low, low)] * (LOW // 16), axis=0)
            tables.append(jnp.where(low == low_at, one, zero))
            high = high_ids[tile, pl.ds(row, 1), :]
            is_high = spread(high, high) == high_at
            kept = []
            for at in range(0, 2 * (COMP + 1), 2):
                pair = spread(
                    split[at, tile, pl.ds(row, 1), :], split[at + 1, tile, pl.ds(row, 1), :]
                )
                kept.append(jnp.where(is_high, pair, zero))
            parts.append(jnp.concatenate(kept, axis=0))
        return total + lax.dot_general(
            jnp.concatenate(parts, axis=1),
            jnp.concatenate(tables, axis=1),
            (((1,), (1,)), ((), ())),
            preferred_element_type=jnp.float32,
        )

    def add_rows(total, start, end, within, together):
        while (end - start) % together:
            together -= 1

        def body(turn, carried):
            todo = [
                (start + turn * together + inner) * cy + row
                for inner in range(together)
                for row in within
            ]
            carried = list(carried)
            for turn_at, first in enumerate(range(0, len(todo), 2)):
                chain = turn_at % CHAINS
                carried[chain] = add_pair(carried[chain], todo[first : first + 2])
            return tuple(carried)

        count = (end - start) // together
        return body(0, total) if count == 1 else lax.fori_loop(0, count, body, total)

    total = (jnp.zeros((PACKED, LOW), jnp.float32),) * CHAINS
    total = add_rows(total, 1, cx - 1, range(1, cy - 1), 2)

    for comp in range(COMP):

        def add_res(side, tile):
            scale = 1.25 * diag[tile, face(side), :] * face_w[side, tile]
            value = split[comp, tile, face(side), :] + split[COMP + 1 + comp, tile, face(side), :]
            value = value + scale * halo_vel[NU - 1, side, comp, tile]
            return lambda: keep_parts(comp, tile, face(side), value)

        with_faces(NU, comp, add_res)

    total = add_rows(total, 1, cx - 1, (0, cy - 1), 14)
    total = add_rows(total, 0, 1, range(cy), 1)
    total = add_rows(total, cx - 1, cx, range(cy), 1)

    total = functools.reduce(jnp.add, total)
    total = total[: PACKED // 2] + total[PACKED // 2 :]
    for comp in range(COMP + 1):
        for half in range(2):
            start = comp * HIGH + half * TILES
            part[comp * TILES : (comp + 1) * TILES, half * LOW : (half + 1) * LOW] = total[
                start : start + TILES
            ]
    part[SUMS : SUMS + 8, :] = jnp.full((8, LANES), own_ref[0, 0], jnp.int32).astype(jnp.float32)

    def share(step):
        return pltpu.make_async_remote_copy(
            src_ref=part,
            dst_ref=gathered.at[step],
            send_sem=all_send.at[step],
            recv_sem=all_recv.at[step],
            device_id=(lax.rem(gx + step, n_gx), gy),
            device_id_type=MESH,
        )

    for step in range(1, n_gx):
        share(step).start()

    base = lax.div(gx, GROUP) * GROUP
    member = lax.broadcasted_iota(jnp.int32, (GROUP, LANES), 0)
    owner_of = (base + member).astype(jnp.float32)
    tiles = [jnp.zeros((GROUP, LANES), jnp.float32) for _ in range(SUMS)]
    for step in range(n_gx):
        if step:
            share(step).wait_recv()
        source = gathered.at[step] if step else part
        mine = source[SUMS : SUMS + 8, :] == owner_of
        for at in range(SUMS):
            row = jnp.broadcast_to(source[at : at + 1, :], (GROUP, LANES))
            tiles[at] = tiles[at] + jnp.where(mine, row, 0.0)
    for at in range(SUMS):
        owned_ref[at] = tiles[at]
    drain(0)
    for turn in range(1, NU + 1):
        for comp in range(COMP):
            drain(turn, comp)
    for step in range(1, n_gx):
        share(step).wait_send()
    for store in stores:
        store.wait()


def coarse_kernel(vel_in, owned_ref, vel_out, cor_ref, sem):
    copies = [
        pltpu.make_async_copy(vel_in.at[comp], vel_out.at[comp], sem.at[comp])
        for comp in range(COMP)
    ]
    for copy in copies:
        copy.start()
    gx = lax.axis_index("gx")
    base = lax.div(gx, GROUP) * GROUP
    owned = [
        jnp.concatenate([owned_ref[comp * TILES + at] for at in range(TILES)], axis=1)
        for comp in range(COMP + 1)
    ]
    coarse_res, coarse_diag = owned[:COMP], 1.0 + owned[COMP]
    lane = lax.broadcasted_iota(jnp.int32, (GROUP, NAGG), 1)
    member = lax.broadcasted_iota(jnp.int32, (GROUP, NAGG), 0)
    own_row = member == gx - base

    def partner(value, level):
        apart = 2**level
        odd = lax.rem(lax.div(member, apart), 2) == 1
        return jnp.where(
            odd, pltpu.roll(value, apart, 0), pltpu.roll(value, GROUP - apart, 0)
        )

    for level in range(MERGES + 1):
        coupling = 0.2 * jnp.minimum(coarse_diag, pltpu.roll(coarse_diag, NAGG - 1, 1))
        coupling = jnp.where(lane == NAGG - 1, 0.0, coupling)
        below = pltpu.roll(coupling, 1, 1)
        scale = 0.8 / coarse_diag

        def left(resid, vector):
            image = (
                coarse_diag * vector
                - coupling * pltpu.roll(vector, NAGG - 1, 1)
                - below * pltpu.roll(vector, 1, 1)
            )
            return resid - image

        merged = []
        for comp in range(COMP):
            resid = coarse_res[comp]
            error = scale * resid
            error = error + scale * left(resid, error)
            cor_ref[0, 0, comp, level : level + 1, :] = jnp.sum(
                jnp.where(own_row, error, 0.0), axis=0, keepdims=True
            )
            if level < MERGES:
                rest = left(resid, error)
                merged.append(rest + partner(rest, level))
        if level < MERGES:
            coarse_res = merged
            coarse_diag = coarse_diag + partner(coarse_diag, level)

    for copy in copies:
        copy.wait()


def shards(n_gx, n_gy, right_side, viscosity, reaction, agg_ids, owner_map):
    comp, cx, cy, cz = right_side.shape
    rows = cx * cy
    whole = (rows, cz)
    tiles_z = cz // LANES
    inside = (tiles_z, rows, LANES)
    rimmed = (tiles_z, rows + 2 * cy, LANES)
    face = (tiles_z, cx, LANES)
    hbm = pl.BlockSpec(memory_space=pltpu.HBM)
    f32 = jnp.float32

    def stay(array):
        return pltpu.with_memory_space_constraint(array, pltpu.HBM)

    velocity, owned = pl.pallas_call(
        functools.partial(kernel, (n_gx, n_gy, cx, cy, cz)),
        out_shape=(
            jax.ShapeDtypeStruct((comp,) + whole, f32),
            jax.ShapeDtypeStruct((SUMS, GROUP, LANES), f32),
        ),
        in_specs=[hbm] * 4 + [pl.BlockSpec(memory_space=pltpu.SMEM)],
        out_specs=(pl.BlockSpec(memory_space=pl.ANY), pl.BlockSpec(memory_space=pltpu.VMEM)),
        scratch_shapes=[
            pltpu.VMEM((comp,) + inside, f32),
            pltpu.VMEM(rimmed, f32),
            pltpu.VMEM(inside, f32),
            pltpu.VMEM(inside, f32),
            pltpu.VMEM(inside, jnp.int32),
            pltpu.VMEM(inside, f32),
            pltpu.VMEM(inside, f32),
            pltpu.VMEM((6,) + inside, f32),
            [pltpu.VMEM((comp,) + rimmed, f32)] * NU,
            pltpu.VMEM((2 * (comp + 1),) + inside, f32),
            pltpu.VMEM((4,) + face, f32),
            pltpu.VMEM((2,) + face, f32),
            pltpu.VMEM((NU, 4, comp) + face, f32),
            pltpu.VMEM((NU, 2, comp) + face, f32),
            pltpu.VMEM((4,) + face, f32),
            pltpu.VMEM((SUMS + 8, LANES), f32),
            pltpu.VMEM((n_gx, SUMS + 8, LANES), f32),
            pltpu.SemaphoreType.DMA((4, tiles_z)),
            pltpu.SemaphoreType.DMA((tiles_z,)),
            pltpu.SemaphoreType.DMA((NU + 1, 4, COMP)),
            pltpu.SemaphoreType.DMA((NU + 1, 4, COMP)),
            pltpu.SemaphoreType.DMA((n_gx,)),
            pltpu.SemaphoreType.DMA((n_gx,)),
        ],
        compiler_params=pltpu.CompilerParams(
            collective_id=0, has_side_effects=True, vmem_limit_bytes=30 * 2**20
        ),
    )(
        stay(right_side.reshape((comp,) + whole)),
        stay(viscosity.reshape(whole)),
        stay(reaction.reshape(whole)),
        stay(agg_ids.reshape(whole)),
        owner_map,
    )
    velocity, levels = pl.pallas_call(
        coarse_kernel,
        out_shape=(
            jax.ShapeDtypeStruct((comp,) + whole, f32),
            jax.ShapeDtypeStruct((1, 1, comp, MERGES + 1, NAGG), f32),
        ),
        in_specs=[pl.BlockSpec(memory_space=pl.ANY), pl.BlockSpec(memory_space=pltpu.VMEM)],
        out_specs=(hbm, pl.BlockSpec(memory_space=pltpu.VMEM)),
        scratch_shapes=[pltpu.SemaphoreType.DMA((COMP,))],
        compiler_params=pltpu.CompilerParams(vmem_limit_bytes=8 * 2**20),
    )(velocity, owned)
    return velocity.reshape(right_side.shape), levels.transpose(0, 1, 3, 2, 4)


def solution(mesh):
    return jax.shard_map(
        functools.partial(shards, mesh.shape["gx"], mesh.shape["gy"]),
        mesh=mesh,
        in_specs=(
            P(None, "gx", "gy", None),
            P("gx", "gy", None),
            P("gx", "gy", None),
            P("gx", "gy", None),
            P("gx", "gy"),
        ),
        out_specs=(P(None, "gx", "gy", None), P("gx", "gy", None, None, None)),
        check_vma=False,
    )
```
